128 devices in a mesh: blk: 32 (over x, y, core), rep: 4 (over z).
Axes of the slice: x: 4, y: 4, z: 4, core: 2. Of those that a mesh axis runs over, the one named last changes fastest.
Arguments:
- tracers: float32 [12, 524288], P(None, 'blk'), may hold values from -6 to 6
- explicit_blocks: bfloat16 [4096, 12, 128, 128], P('blk', 'rep'), may hold values from -0.15625 to 0.15625
- explicit_cols: int32 [4096, 12], P('blk', 'rep'), may hold values from 0 to 4095, as said below
- explicit_sends: int32 [32, 4, 4, 64], P('blk', 'rep'), may hold values from -1 to 127, as said below
- implicit_blocks: bfloat16 [4096, 12, 128, 128], P('blk', 'rep'), may hold values from -0.15625 to 0.15625
- implicit_cols: int32 [4096, 12], P('blk', 'rep'), may hold values from 0 to 4095, as said below
- implicit_sends: int32 [32, 4, 4, 64], P('blk', 'rep'), may hold values from -1 to 127, as said below
- coupling: float32 [12, 12], replicated, may hold values from -1.75 to 1.75
- wet: int32 [524288], P('blk'), may hold values 0 or 1
Outputs:
- updated: float32 [12, 524288], P(None, ('blk', 'rep'))
The draws below stay inside these ranges and needn't reach their ends.
Inputs may be any that keep to these rules, and one draw needn't show every extreme that they name: `explicit_cols`: for block row b on device d = b // 128 and rep index r, slot r * 3 names a block of device d; every other slot of that rep index names a block of a device d' != d with |d' - d| <= 2, listed in that owner's send list for rep index r and direction d - d'. `explicit_sends`: entry (s, r, j, e) is a block index local to device s of a block that device s + o_j reads in its slots of rep index r, with o_j the j-th of -2 .. -1, 1 .. 2; the entries of one list are distinct, used ones first and -1 after them; every listed block is read and every block read from another device is listed; lists toward devices outside the axis are empty; for every sender and rep index one list holds 64 entries. `implicit_cols`: as for explicit_cols, with implicit_sends. `implicit_sends`: as for explicit_sends, for implicit_cols.
All inputs are finite; a program needn't handle non-finite values. No bound on the sum of `wet` on one device may be relied on, other than what follows from the above.
Results may differ from the reference program's by a relative error of at most 0.0029.
Values may be sent and summed in bfloat16 or wider, within the bound.
No kernel may reach another device: no remote copies, remote signals or barrier semaphores. Data moves between devices by JAX's collectives and lax.ppermute only.
A program may use at most 128 MiB of HBM per device.

```python
import jax
import jax.numpy as jnp
from jax import lax

NTR = 12
BS = 128
KE = 12
REACH = 2
NB_DEV = 128
CAP = 64
NB = 4096
CELLS = 524288
N_BLK = 32
N_REP = 4


def offsets_table():
    left_side = jnp.arange(-REACH, 0, dtype=jnp.int32)
    right_side = jnp.arange(1, REACH + 1, dtype=jnp.int32)
    return jnp.concatenate([left_side, right_side])


def block_lists(key, stream_id):
    key = jax.random.fold_in(key, stream_id)
    subkeys = jax.random.split(key, 5)
    lanes = 2 * REACH
    slots_rep = KE // N_REP
    offsets = offsets_table()
    lane_ids = jnp.arange(lanes, dtype=jnp.int32)
    senders = jnp.arange(N_BLK, dtype=jnp.int32)
    target = senders[:, None] + offsets[None, :]
    inside = (target >= 0) & (target < N_BLK)
    counts = jax.random.randint(subkeys[0], (N_BLK, N_REP, lanes), CAP // 2, CAP + 1).astype(jnp.int32)
    scores = jax.random.randint(subkeys[1], (N_BLK, N_REP, lanes), 0, 1000).astype(jnp.int32) * lanes + lane_ids
    scores = jnp.where(inside[:, None, :], scores, -1)
    chosen_lane = jnp.argmax(scores, axis=2).astype(jnp.int32)
    counts = jnp.where(lane_ids[None, None, :] == chosen_lane[:, :, None], CAP, counts)
    counts = jnp.where(inside[:, None, :], counts, 0)
    perm_keys = jax.random.split(subkeys[2], N_BLK * N_REP * lanes)
    shuffled = jax.vmap(lambda subkey: jax.random.permutation(subkey, NB_DEV)[:CAP])(perm_keys)
    shuffled = shuffled.reshape(N_BLK, N_REP, lanes, CAP).astype(jnp.int32)
    slot_ids = jnp.arange(CAP, dtype=jnp.int32)
    sends = jnp.where(slot_ids[None, None, None, :] < counts[..., None], shuffled, -1)
    source = senders[:, None] - offsets[None, :]
    has_source = (source >= 0) & (source < N_BLK)
    clipped = jnp.clip(source, 0, N_BLK - 1)
    lane_grid = jnp.broadcast_to(lane_ids[None, :], (N_BLK, lanes))
    got_counts = counts.transpose(0, 2, 1)[clipped, lane_grid]
    got_counts = jnp.where(has_source[:, :, None], got_counts, 0)
    got_ids = sends.transpose(0, 2, 1, 3)[clipped, lane_grid]
    global_ids = clipped[:, :, None, None] * NB_DEV + got_ids
    recv_counts = got_counts.transpose(0, 2, 1)
    lane_ends = jnp.cumsum(recv_counts, axis=2)
    lane_starts = lane_ends - recv_counts
    listed = lane_ends[:, :, -1]
    remote_count = NB_DEV * (slots_rep - 1)
    order_keys = jax.random.split(subkeys[3], N_BLK * N_REP)
    orders = jax.vmap(lambda subkey: jax.random.permutation(subkey, remote_count))(order_keys)
    orders = orders.reshape(N_BLK, N_REP, remote_count).astype(jnp.int32)
    entry = orders % listed[:, :, None]
    entry_lane = jnp.sum((entry[..., None] >= lane_ends[:, :, None, :]).astype(jnp.int32), axis=-1)
    entry_slot = entry - jnp.take_along_axis(lane_starts, entry_lane, axis=2)
    flat_ids = global_ids.transpose(0, 2, 1, 3).reshape(N_BLK, N_REP, lanes * CAP)
    remote_cols = jnp.take_along_axis(flat_ids, entry_lane * CAP + entry_slot, axis=2)
    remote_cols = remote_cols.reshape(N_BLK, N_REP, NB_DEV, slots_rep - 1)
    local_cols = jax.random.randint(subkeys[4], (N_BLK, N_REP, NB_DEV), 0, NB_DEV).astype(jnp.int32)
    local_cols = local_cols + senders[:, None, None] * NB_DEV
    columns = jnp.concatenate([local_cols[..., None], remote_cols], axis=3)
    columns = columns.transpose(0, 2, 1, 3).reshape(N_BLK * NB_DEV, KE)
    return (columns.astype(jnp.int32), sends.astype(jnp.int32))


def draw_explicit_cols(key, part):
    return block_lists(key, 11)[0]


def draw_explicit_sends(key, part):
    return block_lists(key, 11)[1]


def draw_implicit_cols(key, part):
    return block_lists(key, 23)[0]


def draw_implicit_sends(key, part):
    return block_lists(key, 23)[1]


def set_ends(result, rng, smallest, top_value):
    longest = result.shape.index(max(result.shape))
    spots = []
    for shift in (0, 1):
        where = [jax.random.randint(jax.random.fold_in(rng, axis), (), 0, length) for axis, length in enumerate(result.shape)]
        where[longest] = (where[longest] + shift) % result.shape[longest]
        spots.append(tuple(where))
    return result.at[spots[0]].set(smallest).at[spots[1]].set(top_value)


def block_scale(own_key, dims, shards, smallest, largest):
    def one(position, parts):
        draws = jax.random.uniform(jax.random.fold_in(jax.random.fold_in(own_key, 6), position), (parts,), jnp.float32, smallest / len(shards), largest / len(shards))
        return jnp.repeat(jnp.exp(draws), dims[position] // parts).reshape((-1,) + (1,) * (len(dims) - position - 1))

    gain = one(*shards[0])
    for cut in shards[1:]:
        gain = gain * one(*cut)
    return gain


def gaussian(key, shape, width, most, shards=(), kind=jnp.bfloat16):
    entries = width * jax.random.normal(key, shape, jnp.float32)
    if shards:
        entries = entries * block_scale(key, shape, shards, -0.22, 0.18)
    return jnp.clip(entries, -most, most).astype(kind)


def setup_inputs(seed: int = 0) -> dict:
    arg_keys = jax.random.split(jax.random.key(seed), 10)
    return {
        "tracers": gaussian(arg_keys[0], (NTR, CELLS), 1.0, 6.0, ((1, 32),), jnp.float32),
        "explicit_blocks": gaussian(arg_keys[1], (NB, KE, BS, BS), (BS * KE) ** -0.5, 0.15625, ((0, 32), (1, 4))),
        "explicit_cols": draw_explicit_cols(jax.random.fold_in(arg_keys[9], 71), 0),
        "explicit_sends": draw_explicit_sends(jax.random.fold_in(arg_keys[9], 71), 0),
        "implicit_blocks": gaussian(arg_keys[4], (NB, KE, BS, BS), (BS * KE) ** -0.5, 0.15625, ((0, 32), (1, 4))),
        "implicit_cols": draw_implicit_cols(jax.random.fold_in(arg_keys[9], 71), 0),
        "implicit_sends": draw_implicit_sends(jax.random.fold_in(arg_keys[9], 71), 0),
        "coupling": gaussian(arg_keys[7], (NTR, NTR), NTR ** -0.5, 1.75, (), jnp.float32),
        "wet": set_ends((jax.random.randint(arg_keys[8], (CELLS,), 0, 4) < 3).astype(jnp.int32), jax.random.fold_in(arg_keys[8], 1), 0, 1),
    }


def listed_mask(group_cols, sends, device_rank):
    owners = group_cols // NB_DEV
    local_ids = group_cols - owners * NB_DEV
    rep_of_slot = jnp.arange(KE, dtype=jnp.int32) // (KE // N_REP)
    gap = device_rank - owners
    lane = jnp.where(gap < 0, gap + REACH, gap + REACH - 1)
    lane = jnp.clip(lane, 0, 2 * REACH - 1).astype(jnp.int32)
    near = (gap != 0) & (jnp.abs(gap) <= REACH)
    owner_spot = jnp.clip(owners, 0, N_BLK - 1).astype(jnp.int32)
    rep_grid = jnp.broadcast_to(rep_of_slot[None, :], group_cols.shape)
    lists = sends[owner_spot, rep_grid, lane]
    hit = jnp.any(lists == local_ids[..., None], axis=-1)
    return ((gap == 0) | (near & hit)).astype(jnp.float32)


def apply_blocks(state_b, blocks, columns, sends):
    planes = state_b.reshape(NTR, NB_DEV * N_BLK, BS)

    def apply_group(inputs_triple):
        row_blocks, group_cols, device_rank = inputs_triple
        picked = jnp.take(planes, group_cols.reshape(-1), axis=1)
        picked = picked.reshape(NTR, NB_DEV, KE, BS).astype(jnp.float32)
        keep = listed_mask(group_cols, sends, device_rank)
        picked = picked * keep[None, :, :, None]
        return jnp.einsum("bkij,tbkj->tbi", row_blocks.astype(jnp.float32), picked,
                          precision=lax.Precision.HIGHEST)

    products = lax.map(apply_group, (blocks.reshape(N_BLK, NB_DEV, KE, BS, BS),
                                     columns.reshape(N_BLK, NB_DEV, KE),
                                     jnp.arange(N_BLK, dtype=jnp.int32)))
    return products.transpose(1, 0, 2, 3).reshape(NTR, N_BLK * NB_DEV * BS)


def reference(tracers, explicit_blocks, explicit_cols, explicit_sends, implicit_blocks,
              implicit_cols, implicit_sends, coupling, wet):
    wet_float = wet.astype(jnp.float32)
    state_b = tracers.astype(jnp.bfloat16)
    explicit_sum = apply_blocks(state_b, explicit_blocks, explicit_cols, explicit_sends)
    middle = tracers + explicit_sum
    sources = wet_float[None, :] * jnp.tanh(jnp.dot(coupling, middle, precision=lax.Precision.HIGHEST))
    before = middle + sources
    before_b = before.astype(jnp.bfloat16)
    implicit_sum = apply_blocks(before_b, implicit_blocks, implicit_cols, implicit_sends)
    return wet_float[None, :] * (before + implicit_sum)
```

```python
import functools

import jax
import jax.numpy as jnp
from jax import lax
from jax.experimental import pallas as pl
from jax.experimental.pallas import tpu as pltpu
from jax.sharding import PartitionSpec as P

NTR = 12
BS = 128
NBD = 128
CAP = 64
REP = 4
SHARE = NBD // REP
OFFSETS = (-2, -1, 1, 2)
LIST_ROWS = CAP * NTR
SHARE_ROWS = SHARE * NTR
TABLE = NBD + len(OFFSETS) * CAP
F32 = jnp.float32
BF16 = jnp.bfloat16
I32 = jnp.int32
MIB = 1 << 20

VMEM = pl.BlockSpec(memory_space=pltpu.VMEM)
SMEM = pl.BlockSpec(memory_space=pltpu.SMEM)
ANY = pl.BlockSpec(memory_space=pl.ANY)


def nt(a, b):
    return lax.dot_general(a, b, (((1,), (1,)), ((), ())), preferred_element_type=F32)


def pack4(tiles):
    return jnp.concatenate([t[0:8] for t in tiles] + [t[8:12] for t in tiles], axis=0)


def unpack4(rows):
    return [
        jnp.concatenate([rows[8 * m : 8 * m + 8], rows[32 + 4 * m : 36 + 4 * m]], axis=0)
        for m in range(4)
    ]


def tile16(t):
    return jnp.concatenate([t, jnp.zeros((4, BS), F32)], axis=0).astype(BF16)


def iotas(rows):
    sub = lax.broadcasted_iota(I32, (rows, BS), 0)
    lane = lax.broadcasted_iota(I32, (rows, BS), 1)
    return sub, lane


def before_matrix():
    sub, lane = iotas(BS)
    return jnp.where(sub < lane, 1.0, 0.0).astype(BF16)


def list_order(sends_ref, lane_no):
    entries = sends_ref[lane_no : lane_no + 1, :]
    ids = lax.broadcasted_iota(I32, (BS, CAP), 0)
    hit = jnp.where(ids == entries, 1.0, 0.0).astype(BF16)
    listed = nt(jnp.ones((8, CAP), BF16), hit)
    rank = jnp.dot(listed.astype(BF16), before_matrix(), preferred_element_type=F32)
    spot = lax.broadcasted_iota(I32, (CAP, BS), 0).astype(F32)
    chosen = jnp.where((rank[0:1] == spot) & (listed[0:1] > 0.5), 1.0, 0.0).astype(BF16)
    block = lax.broadcasted_iota(I32, (8, BS), 1).astype(F32).astype(BF16)
    return nt(block, chosen)[0:1].astype(I32)


def table_spots(cols_ref, out_ref, first_block):
    sub, lane = iotas(BS)
    near = lax.broadcasted_iota(I32, (8, BS), 1)
    for row in range(5):
        if row == 2:
            out_ref[row : row + 1, :] = near[0:1]
            continue
        ids = sub + (first_block + row * NBD)
        read = (ids == cols_ref[1:2, :]) | (ids == cols_ref[2:3, :])
        read = jnp.where(read, 1.0, 0.0).astype(BF16)
        read = nt(jnp.ones((8, BS), BF16), read)
        read = jnp.where(read > 0.5, 1.0, 0.0).astype(BF16)
        rank = jnp.dot(read, before_matrix(), preferred_element_type=F32)
        lane_no = OFFSETS.index(2 - row)
        out_ref[row : row + 1, :] = rank[0:1].astype(I32) + (NBD + lane_no * CAP)


def gather_lists(order_ref, load_tile, out_refs):
    for lane_no, out_ref in enumerate(out_refs):

        def group(g, _, lane_no=lane_no, out_ref=out_ref):
            tiles = [load_tile(order_ref[lane_no, 4 * g + m]) for m in range(4)]
            rows = pl.ds(pl.multiple_of(48 * g, 16), 48)
            out_ref[rows, :] = pack4(tiles).astype(BF16)
            return 0

        lax.fori_loop(0, CAP // 4, group, 0, unroll=4)


def first_kernel(sends_ref, tracers_ref, *rest):
    outs, local_ref, order_v, order_s, sem = rest[0:4], rest[4], rest[5], rest[6], rest[7]
    order_v[...] = jnp.zeros((8, BS), I32)
    for lane_no in range(4):
        order_v[lane_no : lane_no + 1, 0:CAP] = list_order(sends_ref, lane_no)
    copy = pltpu.make_async_copy(order_v, order_s, sem)
    copy.start()

    def local(b, _):
        lanes = pl.ds(pl.multiple_of(b * BS, BS), BS)
        local_ref[b] = tile16(tracers_ref[:, lanes])
        return 0

    lax.fori_loop(0, NBD, local, 0, unroll=8)
    copy.wait()

    def load_tile(i):
        return tracers_ref[:, pl.ds(pl.multiple_of(i * BS, BS), BS)]

    gather_lists(order_s, load_tile, outs)


def index_kernel(ecols_ref, icols_ref, isends_ref, espots_ref, ispots_ref, order_ref):
    first_block = (lax.axis_index("blk") - 2) * NBD
    espots_ref[...] = jnp.zeros((8, BS), I32)
    ispots_ref[...] = jnp.zeros((8, BS), I32)
    order_ref[...] = jnp.zeros((8, BS), I32)
    table_spots(ecols_ref, espots_ref, first_block)
    table_spots(icols_ref, ispots_ref, first_block)
    for lane_no in range(4):
        order_ref[lane_no : lane_no + 1, 0:CAP] = list_order(isends_ref, lane_no)


CHUNK = 8


def start_chunks(blocks_ref, held_ref, sems, first_slot, slots, order):
    copies = {}
    for c in order:
        copies[c] = pltpu.make_async_copy(
            blocks_ref.at[pl.ds(c * CHUNK, CHUNK), pl.ds(first_slot, slots)],
            held_ref.at[pl.ds(c * CHUNK, CHUNK)],
            sems.at[c],
        )
        copies[c].start()
    return copies


def local_kernel(cols_ref, table_ref, blocks_ref, out_ref, held_ref, sems):
    base = lax.axis_index("blk") * NBD
    chunks = NBD // CHUNK
    copies = start_chunks(blocks_ref, held_ref, sems, 0, 1, range(chunks))

    for c in range(chunks):
        copies[c].wait()

        def group(g, _):
            tiles = []
            for m in range(4):
                b = 4 * g + m
                tiles.append(nt(table_ref[cols_ref[0, b] - base], held_ref[b, 0]))
            out_ref[pl.ds(pl.multiple_of(48 * g, 16), 48), :] = pack4(tiles)
            return 0

        lax.fori_loop(c * CHUNK // 4, (c + 1) * CHUNK // 4, group, 0, unroll=True)


def remote_kernel(cols_ref, spots_ref, local_ref, blocks_ref, p0, p1, p2, p3,
                  own_ref, o1, o2, o3, held_ref, table_ref, sems):
    me = lax.axis_index("rep")
    first_block = (lax.axis_index("blk") - 2) * NBD
    per_share = SHARE // CHUNK
    copies = []
    for step in (2, 1, 3, 0):
        share = lax.rem(me + step, REP)
        for part in range(per_share):
            b0 = (share * per_share + part) * CHUNK
            slot = len(copies)
            copies.append(pltpu.make_async_copy(
                blocks_ref.at[pl.ds(b0, CHUNK), pl.ds(1, 2)],
                held_ref.at[pl.ds(slot * CHUNK, CHUNK)],
                sems.at[slot],
            ))
            copies[-1].start()

    for lane_no, piece in enumerate((p0, p1, p2, p3)):

        def spread(g, _, lane_no=lane_no, piece=piece):
            rows = piece[pl.ds(pl.multiple_of(48 * g, 16), 48), :].astype(F32)
            for m, tile in enumerate(unpack4(rows)):
                table_ref[lane_no * CAP + 4 * g + m] = tile16(tile)
            return 0

        lax.fori_loop(0, CAP // 4, spread, 0, unroll=4)

    def spot(k, b):
        c = cols_ref[k, b] - first_block
        return spots_ref[lax.shift_right_logical(c, 7), c & (NBD - 1)] - NBD

    slot = 0
    for step, out_ref in ((2, o2), (1, o1), (3, o3), (0, own_ref)):
        share = lax.rem(me + step, REP)
        for part in range(per_share):
            copies[slot].wait()

            def group(g, _, part=part, slot=slot, out_ref=out_ref, share=share):
                tiles = []
                for m in range(4):
                    row = 4 * g + m
                    b = share * SHARE + part * CHUNK + row
                    x = jnp.concatenate([table_ref[spot(1, b)], table_ref[spot(2, b)]], axis=1)
                    h = slot * CHUNK + row
                    w = jnp.concatenate([held_ref[h, 0], held_ref[h, 1]], axis=1)
                    tiles.append(nt(x, w))
                at = part * (CHUNK // 4) + g
                there = pl.ds(pl.multiple_of((share * (SHARE // 4) + at) * 48, 16), 48)
                total = pack4(tiles) + local_ref[there, :]
                out_ref[pl.ds(pl.multiple_of(48 * at, 16), 48), :] = total.astype(out_ref.dtype)
                return 0

            lax.fori_loop(0, CHUNK // 4, group, 0, unroll=True)
            slot += 1


def middle_kernel(own_ref, g1, g2, g3, tracers_ref, coupling_ref, wet_ref,
                  before_ref, packed_ref, tr_ref, wet_v, mid_ref, sems):
    me = lax.axis_index("rep")
    cells = SHARE * BS
    c1 = pltpu.make_async_copy(
        tracers_ref.at[:, pl.ds(pl.multiple_of(me * cells, cells), cells)], tr_ref, sems.at[0])
    c1.start()
    c2 = pltpu.make_async_copy(
        wet_ref.at[pl.ds(pl.multiple_of(me * SHARE, SHARE), SHARE)], wet_v, sems.at[1])
    c2.start()
    c1.wait()
    c2.wait()
    mid_ref[NTR:16, :] = jnp.zeros((16 - NTR, cells), F32)
    for g in range(SHARE // 4):
        rows = pl.ds(48 * g, 48)
        total = own_ref[rows, :] + g1[rows, :].astype(F32) + g2[rows, :].astype(F32) + g3[rows, :].astype(F32)
        for m, tile in enumerate(unpack4(total)):
            lanes = pl.ds((4 * g + m) * BS, BS)
            mid_ref[0:NTR, lanes] = tr_ref[:, lanes] + tile
    pushed = lax.dot_general(coupling_ref[...], mid_ref[...], (((1,), (0,)), ((), ())),
                             precision=lax.Precision.HIGHEST, preferred_element_type=F32)
    for g in range(SHARE // 4):
        tiles = []
        for m in range(4):
            b = 4 * g + m
            lanes = pl.ds(b * BS, BS)
            wet = wet_v[b : b + 1, :].astype(F32)
            tile = mid_ref[0:NTR, lanes] + wet * jnp.tanh(pushed[0:NTR, b * BS : (b + 1) * BS])
            before_ref[:, lanes] = tile
            tiles.append(tile)
        packed_ref[pl.ds(48 * g, 48), :] = pack4(tiles).astype(BF16)


def second_kernel(order_ref, own, g1, g2, g3, *rest):
    outs, table_ref = rest[0:4], rest[4]
    me = lax.axis_index("rep")
    for step, packed in enumerate((own, g1, g2, g3)):
        share = lax.rem(me - step + REP, REP)

        def spread(g, _, packed=packed, share=share):
            rows = packed[pl.ds(pl.multiple_of(48 * g, 16), 48), :].astype(F32)
            for m, tile in enumerate(unpack4(rows)):
                table_ref[share * SHARE + 4 * g + m] = tile16(tile)
            return 0

        lax.fori_loop(0, SHARE // 4, spread, 0, unroll=4)
    gather_lists(order_ref, lambda i: table_ref[i].astype(F32), outs)


def last_kernel(own_ref, g1, g2, g3, before_ref, wet_ref, out_ref, wet_v, sem):
    me = lax.axis_index("rep")
    copy = pltpu.make_async_copy(
        wet_ref.at[pl.ds(pl.multiple_of(me * SHARE, SHARE), SHARE)], wet_v, sem)
    copy.start()
    copy.wait()
    for g in range(SHARE // 4):
        rows = pl.ds(48 * g, 48)
        total = own_ref[rows, :] + g1[rows, :].astype(F32) + g2[rows, :].astype(F32) + g3[rows, :].astype(F32)
        for m, tile in enumerate(unpack4(total)):
            b = 4 * g + m
            lanes = pl.ds(b * BS, BS)
            wet = wet_v[b : b + 1, :].astype(F32)
            out_ref[:, lanes] = wet * (before_ref[:, lanes] + tile)


def sds(shape, dtype):
    return jax.ShapeDtypeStruct(shape, dtype)


def call(body, outs, in_specs, scratch, name, mib, flops=0, bytes_accessed=0):
    return pl.pallas_call(
        body,
        out_shape=outs,
        in_specs=in_specs,
        out_specs=jax.tree.map(lambda _: VMEM, outs),
        scratch_shapes=scratch,
        compiler_params=pltpu.CompilerParams(vmem_limit_bytes=mib * MIB),
        cost_estimate=pl.CostEstimate(flops=flops, bytes_accessed=bytes_accessed, transcendentals=0),
        name=name,
    )


def shift_blk(x, distance):
    n = lax.axis_size("blk")
    return lax.ppermute(x, "blk", [(i - distance, i) for i in range(n) if 0 <= i - distance < n])


def shift_rep(x, distance):
    n = lax.axis_size("rep")
    return lax.ppermute(x, "rep", [(i, (i + distance) % n) for i in range(n)])


def lists_out():
    return [sds((LIST_ROWS, BS), BF16)] * 4


def products(cols, spots, table, blocks, pieces):
    local = call(
        local_kernel, sds((NBD * NTR, BS), F32), [SMEM, VMEM, ANY],
        [pltpu.VMEM((NBD, 1, BS, BS), BF16), pltpu.SemaphoreType.DMA((NBD // CHUNK,))],
        "local_product", 16, flops=50_000_000, bytes_accessed=5_000_000,
    )(cols, table, blocks)
    share = sds((SHARE_ROWS, BS), BF16)
    return call(
        remote_kernel, [sds((SHARE_ROWS, BS), F32), share, share, share],
        [SMEM, SMEM, VMEM, ANY, VMEM, VMEM, VMEM, VMEM],
        [pltpu.VMEM((NBD, 2, BS, BS), BF16), pltpu.VMEM((4 * CAP, 16, BS), BF16),
         pltpu.SemaphoreType.DMA((NBD // CHUNK,))],
        "remote_product", 24, flops=100_000_000, bytes_accessed=10_000_000,
    )(cols, spots, local, blocks, *pieces)


def on_device(tracers, explicit_blocks, explicit_cols, explicit_sends,
              implicit_blocks, implicit_cols, implicit_sends, coupling, wet):
    ecols, icols = explicit_cols.T, implicit_cols.T
    esends, isends = explicit_sends.reshape(4, CAP), implicit_sends.reshape(4, CAP)
    wet = wet.reshape(NBD, BS)
    coupling = jnp.pad(coupling, ((0, 4), (0, 4)))
    cells = SHARE * BS

    *outbound, table = call(
        first_kernel, lists_out() + [sds((NBD, 16, BS), BF16)], [VMEM, VMEM],
        [pltpu.VMEM((8, BS), I32), pltpu.SMEM((8, BS), I32), pltpu.SemaphoreType.DMA],
        "first_lists", 16,
    )(esends, tracers)
    espots, ispots, iorder = call(
        index_kernel, [sds((8, BS), I32)] * 3, [VMEM, VMEM, VMEM], [], "indices", 8,
    )(ecols, icols, isends)
    pieces = [shift_blk(x, o) for x, o in zip(outbound, OFFSETS)]
    own, *parts = products(ecols, espots, table, explicit_blocks, pieces)
    got = [shift_rep(x, k + 1) for k, x in enumerate(parts)]
    before, packed = call(
        middle_kernel, [sds((NTR, cells), F32), sds((SHARE_ROWS, BS), BF16)],
        [VMEM, VMEM, VMEM, VMEM, ANY, VMEM, ANY],
        [pltpu.VMEM((NTR, cells), F32), pltpu.VMEM((SHARE, BS), I32),
         pltpu.VMEM((16, cells), F32), pltpu.SemaphoreType.DMA((2,))],
        "middle", 16,
    )(own, *got, tracers, coupling, wet)
    others = [shift_rep(packed, k) for k in (1, 2, 3)]
    *outbound, table = call(
        second_kernel, lists_out() + [sds((NBD, 16, BS), BF16)], [SMEM] + [VMEM] * 4, [],
        "second_lists", 16,
    )(iorder, packed, *others)
    pieces = [shift_blk(x, o) for x, o in zip(outbound, OFFSETS)]
    own, *parts = products(icols, ispots, table, implicit_blocks, pieces)
    got = [shift_rep(x, k + 1) for k, x in enumerate(parts)]
    return call(
        last_kernel, sds((NTR, cells), F32), [VMEM] * 5 + [ANY],
        [pltpu.VMEM((SHARE, BS), I32), pltpu.SemaphoreType.DMA], "last", 16,
    )(own, *got, before, wet)


def solution(mesh):
    in_specs = (
        P(None, "blk"),
        P("blk", "rep", None, None),
        P("blk", "rep"),
        P("blk", "rep", None, None),
        P("blk", "rep", None, None),
        P("blk", "rep"),
        P("blk", "rep", None, None),
        P(),
        P("blk"),
    )
    out_specs = P(None, ("blk", "rep"))
    return jax.shard_map(
        on_device, mesh=mesh, in_specs=in_specs, out_specs=out_specs, check_vma=False
    )
```

```python
import jax
import jax.numpy as jnp
from jax import lax
from jax.experimental import pallas as pl
from jax.experimental.pallas import tpu as pltpu
from jax.sharding import PartitionSpec as P

NTR = 12
BS = 128
NBD = 128
CAP = 64
REP = 4
SHARE = NBD // REP
LIST_ROWS = CAP * NTR
SHARE_ROWS = SHARE * NTR
F32 = jnp.float32
BF16 = jnp.bfloat16
I32 = jnp.int32
MIB = 1 << 20

VMEM = pl.BlockSpec(memory_space=pltpu.VMEM)
SMEM = pl.BlockSpec(memory_space=pltpu.SMEM)
HBM = pl.BlockSpec(memory_space=pltpu.HBM)


def nt(a, b):
    return lax.dot_general(a, b, (((1,), (1,)), ((), ())), preferred_element_type=F32)


def pack4(tiles):
    return jnp.concatenate([t[0:8] for t in tiles] + [t[8:12] for t in tiles], axis=0)


def unpack4(rows):
    return [
        jnp.concatenate([rows[8 * m : 8 * m + 8], rows[32 + 4 * m : 36 + 4 * m]], axis=0)
        for m in range(4)
    ]


def tile16(t):
    return jnp.concatenate([t, jnp.zeros((4, BS), F32)], axis=0).astype(BF16)


def iotas(rows):
    sub = lax.broadcasted_iota(I32, (rows, BS), 0)
    lane = lax.broadcasted_iota(I32, (rows, BS), 1)
    return sub, lane


def before_matrix():
    sub, lane = iotas(BS)
    return jnp.where(sub < lane, 1.0, 0.0).astype(BF16)


def list_order(sends_ref, lane_no):
    entries = sends_ref[lane_no : lane_no + 1, :]
    ids = lax.broadcasted_iota(I32, (BS, CAP), 0)
    hit = jnp.where(ids == entries, 1.0, 0.0).astype(BF16)
    listed = nt(jnp.ones((8, CAP), BF16), hit)
    rank = jnp.dot(listed.astype(BF16), before_matrix(), preferred_element_type=F32)
    spot = lax.broadcasted_iota(I32, (CAP, BS), 0).astype(F32)
    chosen = jnp.where((rank[0:1] == spot) & (listed[0:1] > 0.5), 1.0, 0.0).astype(BF16)
    block = lax.broadcasted_iota(I32, (8, BS), 1).astype(F32).astype(BF16)
    return nt(block, chosen)[0:1].astype(I32)


def route_lanes():
    me = lax.axis_index("blk")
    core = me & 1
    odd = lax.shift_right_logical(me, 1) & 1
    return (2 - core, 1 + core, 3 * odd, 3 - 3 * odd)


def table_spots(cols_ref, out_ref, first_block):
    sub, lane = iotas(BS)
    me = lax.axis_index("blk")
    core = me & 1
    odd = lax.shift_right_logical(me, 1) & 1
    message = {0: 2 + odd, 1: 1 - core, 3: core, 4: 3 - odd}
    out_ref[2:3, :] = lane[0:1]
    for row in (0, 1, 3, 4):
        ids = sub + (first_block + row * NBD)
        read = (ids == cols_ref[1:2, :]) | (ids == cols_ref[2:3, :])
        read = jnp.where(read, 1.0, 0.0).astype(BF16)
        read = nt(jnp.ones((8, BS), BF16), read)
        read = jnp.where(read > 0.5, 1.0, 0.0).astype(BF16)
        rank = jnp.dot(read, before_matrix(), preferred_element_type=F32)
        out_ref[row : row + 1, :] = rank[0:1].astype(I32) + message[row] * CAP


def gather_lists(order_ref, load_tile, out_refs):
    for lane_no, out_ref in zip(route_lanes(), out_refs):

        def group(g, _, lane_no=lane_no, out_ref=out_ref):
            tiles = [load_tile(order_ref[lane_no, 4 * g + m]) for m in range(4)]
            rows = pl.ds(pl.multiple_of(48 * g, 16), 48)
            out_ref[rows, :] = pack4(tiles).astype(BF16)
            return 0

        lax.fori_loop(0, CAP // 4, group, 0, unroll=4)


def fetch(pairs, sems):
    copies = [pltpu.make_async_copy(src, dst, sems.at[n]) for n, (src, dst) in enumerate(pairs)]
    for copy in copies:
        copy.start()
    return copies


def first_kernel(sends_ref, tracers_ref, *rest):
    outs = rest[0:4]
    sends_v, tracers_v, order_v, order_s, sems, sem = rest[4:]
    copies = fetch([(sends_ref, sends_v), (tracers_ref, tracers_v)], sems)
    order_v[...] = jnp.zeros((8, BS), I32)
    copies[0].wait()
    for lane_no in range(4):
        order_v[lane_no : lane_no + 1, 0:CAP] = list_order(sends_v, lane_no)
    copy = pltpu.make_async_copy(order_v, order_s, sem)
    copy.start()
    copies[1].wait()
    copy.wait()

    def load_tile(i):
        return tracers_v[:, pl.ds(pl.multiple_of(i * BS, BS), BS)]

    gather_lists(order_s, load_tile, outs)


def fetch_local(blocks_ref, held_ref, sems):
    return fetch(
        [(blocks_ref.at[pl.ds(q * SHARE, SHARE), pl.ds(0, 1)], held_ref.at[pl.ds(q * SHARE, SHARE)])
         for q in range(REP)], sems)


def local_groups(copies, cols_s, load_tile, held_ref, out_ref):
    base = lax.axis_index("blk") * NBD
    for q in range(REP):
        copies[q].wait()

        def group(g, _):
            tiles = []
            for m in range(4):
                b = 4 * g + m
                tiles.append(nt(load_tile(cols_s[0, b] - base), held_ref[b, 0]))
            out_ref[pl.ds(pl.multiple_of(48 * g, 16), 48), :] = pack4(tiles)
            return 0

        lax.fori_loop(q * SHARE // 4, (q + 1) * SHARE // 4, group, 0, unroll=True)


def first_local_kernel(ecols_ref, icols_ref, isends_ref, tracers_ref, wet_ref, blocks_ref,
                       out_ref, espots_ref, ispots_ref, order_ref, share_ref, wet_share_ref,
                       ecols_v, icols_v, isends_v, wet_v, ecols_s, tracers_v, held_ref, sems, block_sems):
    me = lax.axis_index("rep")
    first_block = (lax.axis_index("blk") - 2) * NBD
    cells = SHARE * BS
    copies = fetch([
        (ecols_ref, ecols_v), (icols_ref, icols_v), (isends_ref, isends_v), (ecols_ref, ecols_s),
        (tracers_ref, tracers_v),
        (tracers_ref.at[:, pl.ds(pl.multiple_of(me * cells, cells), cells)], share_ref),
        (wet_ref.at[pl.ds(pl.multiple_of(me * SHARE, SHARE), SHARE)], wet_v),
    ], sems)
    block_copies = fetch_local(blocks_ref, held_ref, block_sems)
    for ref in (espots_ref, ispots_ref, order_ref):
        ref[...] = jnp.zeros((8, BS), I32)
    for copy in copies:
        copy.wait()
    wet_share_ref[...] = wet_v[...].astype(F32)
    table_spots(ecols_v, espots_ref, first_block)
    table_spots(icols_v, ispots_ref, first_block)
    for lane_no in range(4):
        order_ref[lane_no : lane_no + 1, 0:CAP] = list_order(isends_v, lane_no)

    def load_tile(i):
        return tile16(tracers_v[:, pl.ds(pl.multiple_of(i * BS, BS), BS)])

    local_groups(block_copies, ecols_s, load_tile, held_ref, out_ref)


def second_local_kernel(cols_ref, table_ref, blocks_ref, out_ref, cols_s, held_ref, sems, block_sems):
    copies = fetch([(cols_ref, cols_s)], sems)
    block_copies = fetch_local(blocks_ref, held_ref, block_sems)
    copies[0].wait()
    local_groups(block_copies, cols_s, lambda i: table_ref[i], held_ref, out_ref)


def remote_kernel(cols_ref, spots_ref, local_ref, blocks_ref, p0, p1, p2, p3,
                  own_ref, o1, o2, o3, cols_s, held_ref, table_ref, sems, block_sems):
    me = lax.axis_index("rep")
    first_block = (lax.axis_index("blk") - 2) * NBD
    steps = ((1, o1), (3, o3), (2, o2), (0, own_ref))
    shares = [me ^ step for step, _ in steps]
    copies = fetch([(cols_ref, cols_s)], sems)
    block_copies = fetch(
        [(blocks_ref.at[pl.ds(share * SHARE, SHARE), pl.ds(1, 2)], held_ref.at[pl.ds(n * SHARE, SHARE)])
         for n, share in enumerate(shares)], block_sems)

    for lane_no, piece in enumerate((p0, p1, p2, p3)):

        def spread(g, _, lane_no=lane_no, piece=piece):
            rows = piece[pl.ds(pl.multiple_of(48 * g, 16), 48), :].astype(F32)
            for m, tile in enumerate(unpack4(rows)):
                table_ref[lane_no * CAP + 4 * g + m] = tile16(tile)
            return 0

        lax.fori_loop(0, CAP // 4, spread, 0, unroll=4)

    def tile(k, b):
        c = cols_s[k, b] - first_block
        return table_ref[spots_ref[lax.shift_right_logical(c, 7), c & (NBD - 1)]]

    copies[0].wait()
    for n, (_, out_ref) in enumerate(steps):
        share = shares[n]
        block_copies[n].wait()

        def group(g, _, n=n, out_ref=out_ref, share=share):
            tiles = []
            for pair in range(2):
                xs, ws = [], []
                for half in range(2):
                    row = 4 * g + 2 * pair + half
                    b = share * SHARE + row
                    h = n * SHARE + row
                    xs.append(jnp.concatenate([tile(1, b), tile(2, b)], axis=1))
                    ws.append(jnp.concatenate([held_ref[h, 0], held_ref[h, 1]], axis=1))
                y = nt(jnp.concatenate(xs, axis=0), jnp.concatenate(ws, axis=0))
                tiles += [y[0:16, 0:BS], y[16:32, BS:]]
            there = pl.ds(pl.multiple_of((share * (SHARE // 4) + g) * 48, 16), 48)
            total = pack4(tiles) + local_ref[there, :]
            out_ref[pl.ds(pl.multiple_of(48 * g, 16), 48), :] = total.astype(out_ref.dtype)
            return 0

        lax.fori_loop(0, SHARE // 4, group, 0, unroll=True)


def middle_kernel(own_ref, g1, g2, g3, share_ref, coupling_ref, wet_ref,
                  before_ref, packed_ref, coupling_v, mid_ref, sem):
    copy = pltpu.make_async_copy(coupling_ref, coupling_v, sem)
    copy.start()
    for g in range(SHARE // 4):
        rows = pl.ds(48 * g, 48)
        total = own_ref[rows, :] + g1[rows, :].astype(F32) + g2[rows, :].astype(F32) + g3[rows, :].astype(F32)
        for m, tile in enumerate(unpack4(total)):
            lanes = pl.ds((4 * g + m) * BS, BS)
            mid_ref[:, lanes] = share_ref[:, lanes] + tile
    copy.wait()
    pushed = lax.dot_general(coupling_v[...], mid_ref[...], (((1,), (0,)), ((), ())),
                             precision=lax.Precision.HIGHEST, preferred_element_type=F32)
    for g in range(SHARE // 4):
        tiles = []
        for m in range(4):
            b = 4 * g + m
            lanes = pl.ds(b * BS, BS)
            tile = mid_ref[:, lanes] + wet_ref[b : b + 1, :] * jnp.tanh(pushed[:, b * BS : (b + 1) * BS])
            before_ref[:, lanes] = tile
            tiles.append(tile)
        packed_ref[pl.ds(48 * g, 48), :] = pack4(tiles).astype(BF16)


def second_kernel(order_ref, own, g2, g3, g1, *rest):
    outs, table_ref = rest[0:4], rest[4]
    me = lax.axis_index("rep")
    for step, packed in ((0, own), (2, g2), (3, g3), (1, g1)):
        share = me ^ step

        def spread(g, _, packed=packed, share=share):
            rows = packed[pl.ds(pl.multiple_of(48 * g, 16), 48), :].astype(F32)
            for m, tile in enumerate(unpack4(rows)):
                table_ref[share * SHARE + 4 * g + m] = tile16(tile)
            return 0

        lax.fori_loop(0, SHARE // 4, spread, 0, unroll=4)
    gather_lists(order_ref, lambda i: table_ref[i].astype(F32), outs)


def last_kernel(own_ref, g1, g2, g3, before_ref, wet_ref, out_ref):
    for g in range(SHARE // 4):
        rows = pl.ds(48 * g, 48)
        total = own_ref[rows, :] + g1[rows, :].astype(F32) + g2[rows, :].astype(F32) + g3[rows, :].astype(F32)
        for m, tile in enumerate(unpack4(total)):
            b = 4 * g + m
            lanes = pl.ds(b * BS, BS)
            out_ref[:, lanes] = wet_ref[b : b + 1, :] * (before_ref[:, lanes] + tile)


def sds(shape, dtype):
    return jax.ShapeDtypeStruct(shape, dtype)


def call(body, outs, in_specs, scratch, name, mib, flops=0, bytes_accessed=0):
    kernel = pl.pallas_call(
        body,
        out_shape=outs,
        in_specs=in_specs,
        out_specs=jax.tree.map(lambda _: VMEM, outs),
        scratch_shapes=scratch,
        compiler_params=pltpu.CompilerParams(vmem_limit_bytes=mib * MIB),
        cost_estimate=pl.CostEstimate(flops=flops, bytes_accessed=bytes_accessed, transcendentals=0),
        name=name,
    )

    def run(*operands):
        return kernel(*(
            pltpu.with_memory_space_constraint(x, pltpu.HBM) if spec is HBM else x
            for x, spec in zip(operands, in_specs)))

    return run


def swap_blk(messages):
    n = lax.axis_size("blk")
    partners = (
        lambda i: i ^ 1,
        lambda i: i + 1 if i & 1 else i - 1,
        lambda i: i + 2 if i & 2 else i - 2,
        lambda i: i ^ 2,
    )
    return [
        lax.ppermute(x, "blk", [(i, to(i)) for i in range(n) if 0 <= to(i) < n])
        for x, to in zip(messages, partners)
    ]


def swap_rep(x, distance):
    n = lax.axis_size("rep")
    return lax.ppermute(x, "rep", [(i, i ^ distance) for i in range(n)])


def lists_out():
    return [sds((LIST_ROWS, BS), BF16)] * 4


def dma(n):
    return pltpu.SemaphoreType.DMA((n,))


def held(slots):
    return pltpu.VMEM((NBD, slots, BS, BS), BF16)


def remote_product(cols, spots, local, blocks, pieces):
    share = sds((SHARE_ROWS, BS), BF16)
    return call(
        remote_kernel, [sds((SHARE_ROWS, BS), F32), share, share, share],
        [HBM, SMEM, VMEM, HBM, VMEM, VMEM, VMEM, VMEM],
        [pltpu.SMEM((3, BS), I32), held(2), pltpu.VMEM((4 * CAP, 16, BS), BF16), dma(1), dma(REP)],
        "remote_product", 24, flops=100_000_000, bytes_accessed=10_000_000,
    )(cols, spots, local, blocks, *pieces)


def on_device(tracers, explicit_blocks, explicit_cols, explicit_sends,
              implicit_blocks, implicit_cols, implicit_sends, coupling, wet):
    ecols, icols = explicit_cols.T, implicit_cols.T
    esends, isends = explicit_sends.reshape(4, CAP), implicit_sends.reshape(4, CAP)
    wet = wet.reshape(NBD, BS)
    cells = SHARE * BS
    ints = sds((8, BS), I32)
    small = pltpu.VMEM((3, BS), I32)
    local_sum = sds((NBD * NTR, BS), F32)

    outbound = call(
        first_kernel, lists_out(), [HBM, HBM],
        [pltpu.VMEM((4, CAP), I32), pltpu.VMEM((NTR, NBD * BS), F32), pltpu.VMEM((8, BS), I32),
         pltpu.SMEM((8, BS), I32), dma(2), pltpu.SemaphoreType.DMA],
        "first_lists", 16,
    )(esends, tracers)
    pieces = swap_blk(outbound)
    local, espots, ispots, iorder, share, wet_share = call(
        first_local_kernel,
        [local_sum, ints, ints, ints, sds((NTR, cells), F32), sds((SHARE, BS), F32)], [HBM] * 6,
        [small, small, pltpu.VMEM((4, CAP), I32), pltpu.VMEM((SHARE, BS), I32), pltpu.SMEM((3, BS), I32),
         pltpu.VMEM((NTR, NBD * BS), F32), held(1), dma(7), dma(REP)],
        "first_local_product", 20, flops=50_000_000, bytes_accessed=5_000_000,
    )(ecols, icols, isends, tracers, wet, explicit_blocks)
    own, *parts = remote_product(ecols, espots, local, explicit_blocks, pieces)
    got = [swap_rep(parts[k - 1], k) for k in (1, 3, 2)]
    before, packed = call(
        middle_kernel, [sds((NTR, cells), F32), sds((SHARE_ROWS, BS), BF16)],
        [VMEM, VMEM, VMEM, VMEM, VMEM, HBM, VMEM],
        [pltpu.VMEM((NTR, NTR), F32), pltpu.VMEM((NTR, cells), F32), pltpu.SemaphoreType.DMA],
        "middle", 16,
    )(own, *got, share, coupling, wet_share)
    others = [swap_rep(packed, k) for k in (2, 3, 1)]
    *outbound, table = call(
        second_kernel, lists_out() + [sds((NBD, 16, BS), BF16)], [SMEM] + [VMEM] * 4, [],
        "second_lists", 16,
    )(iorder, packed, *others)
    pieces = swap_blk(outbound)
    local = call(
        second_local_kernel, local_sum, [HBM, VMEM, HBM],
        [pltpu.SMEM((3, BS), I32), held(1), dma(1), dma(REP)],
        "second_local_product", 16, flops=50_000_000, bytes_accessed=5_000_000,
    )(icols, table, implicit_blocks)
    own, *parts = remote_product(icols, ispots, local, implicit_blocks, pieces)
    got = [swap_rep(parts[k - 1], k) for k in (1, 3, 2)]
    return call(
        last_kernel, sds((NTR, cells), F32), [VMEM] * 6, [], "last", 16,
    )(own, *got, before, wet_share)


def solution(mesh):
    in_specs = (
        P(None, "blk"),
        P("blk", "rep", None, None),
        P("blk", "rep"),
        P("blk", "rep", None, None),
        P("blk", "rep", None, None),
        P("blk", "rep"),
        P("blk", "rep", None, None),
        P(),
        P("blk"),
    )
    out_specs = P(None, ("blk", "rep"))
    return jax.shard_map(
        on_device, mesh=mesh, in_specs=in_specs, out_specs=out_specs, check_vma=False
    )
```

```python
import jax
import jax.numpy as jnp
from jax import lax
from jax.experimental import pallas as pl
from jax.experimental.pallas import tpu as pltpu
from jax.sharding import PartitionSpec as P

NTR = 12
BS = 128
NBD = 128
CAP = 64
REP = 4
SHARE = NBD // REP
LIST_ROWS = CAP * NTR
LABEL_ROWS = 16
SHARE_ROWS = SHARE * NTR
F32 = jnp.float32
BF16 = jnp.bfloat16
I32 = jnp.int32
MIB = 1 << 20

VMEM = pl.BlockSpec(memory_space=pltpu.VMEM)
HBM = pl.BlockSpec(memory_space=pltpu.HBM)


def nt(a, b):
    return lax.dot_general(a, b, (((1,), (1,)), ((), ())), preferred_element_type=F32)


def pack4(tiles):
    return jnp.concatenate([t[0:8] for t in tiles] + [t[8:12] for t in tiles], axis=0)


def unpack4(rows):
    return [
        jnp.concatenate([rows[8 * m : 8 * m + 8], rows[32 + 4 * m : 36 + 4 * m]], axis=0)
        for m in range(4)
    ]


def tile16(t):
    return jnp.concatenate([t, jnp.zeros((4, BS), F32)], axis=0).astype(BF16)


def route_lanes():
    me = lax.axis_index("blk")
    core = me & 1
    odd = lax.shift_right_logical(me, 1) & 1
    return (2 - core, 1 + core, 3 * odd, 3 - 3 * odd)


def message_spots(pieces, espots_ref, ispots_ref):
    me = lax.axis_index("blk")
    core = me & 1
    odd = lax.shift_right_logical(me, 1) & 1
    sub = lax.broadcasted_iota(I32, (BS, BS), 0).astype(F32)
    spot = lax.broadcasted_iota(I32, (8, BS), 1)
    kind = lax.broadcasted_iota(I32, (8, BS), 0)
    spot = jnp.where(lax.shift_right_logical(spot, 6) == kind, spot & (CAP - 1), 0)
    spot = spot.astype(F32).astype(BF16)
    for n, row in enumerate((3 - 2 * core, 1 + 2 * core, 4 * odd, 4 - 4 * odd)):
        labels = pieces[n][LIST_ROWS : LIST_ROWS + LABEL_ROWS, :].astype(F32)[0:1]
        listed = jnp.where(sub == labels, 1.0, 0.0).astype(BF16)
        found = nt(spot, listed).astype(I32) + n * CAP
        espots_ref[pl.ds(row, 1), :] = found[0:1]
        ispots_ref[pl.ds(row, 1), :] = found[1:2]


def gather_lists(order_ref, load_tile, out_refs):
    for lane_no, out_ref in zip(route_lanes(), out_refs):

        def group(g, _, lane_no=lane_no, out_ref=out_ref):
            tiles = [load_tile(jnp.maximum(order_ref[lane_no, 4 * g + m], 0)) for m in range(4)]
            rows = pl.ds(pl.multiple_of(48 * g, 16), 48)
            out_ref[rows, :] = pack4(tiles).astype(BF16)
            return 0

        lax.fori_loop(0, CAP // 4, group, 0, unroll=4)


def fetch(pairs, sems):
    copies = [pltpu.make_async_copy(src, dst, sems.at[n]) for n, (src, dst) in enumerate(pairs)]
    for copy in copies:
        copy.start()
    return copies


def first_kernel(esends_ref, isends_ref, tracers_ref, *rest):
    outs = rest[0:4]
    esends_v, isends_v, esends_s, tracers_v, sems = rest[4:]
    copies = fetch([(esends_ref, esends_s), (tracers_ref, tracers_v),
                    (esends_ref, esends_v), (isends_ref, isends_v)], sems)
    for copy in copies:
        copy.wait()
    for lane_no, out_ref in zip(route_lanes(), outs):
        row = pl.ds(lane_no, 1)
        labels = jnp.concatenate([esends_v[row, :], isends_v[row, :]], axis=1).astype(F32)
        out_ref[LIST_ROWS : LIST_ROWS + LABEL_ROWS, :] = jnp.broadcast_to(labels, (LABEL_ROWS, BS)).astype(BF16)

    def load_tile(i):
        return tracers_v[:, pl.ds(pl.multiple_of(i * BS, BS), BS)]

    gather_lists(esends_s, load_tile, outs)


def fetch_blocks(blocks_ref, near_ref, far_ref, sems):
    rows = [pl.ds(q * SHARE, SHARE) for q in range(REP)]
    return fetch([(blocks_ref.at[r, pl.ds(0, 1)], near_ref.at[r]) for r in rows]
                 + [(blocks_ref.at[r, pl.ds(1, 2)], far_ref.at[r]) for r in rows], sems)


def local_groups(copies, cols_s, load_tile, near_ref, out_ref):
    base = lax.axis_index("blk") * NBD
    for q in range(REP):
        copies[q].wait()

        def group(g, _):
            tiles = []
            for pair in range(2):
                bs = [4 * g + 2 * pair + half for half in range(2)]
                x = jnp.concatenate([load_tile(cols_s[0, b] - base) for b in bs], axis=0)
                w = jnp.concatenate([near_ref[b, 0] for b in bs], axis=0)
                y = nt(x, w)
                tiles += [y[0:16, 0:BS], y[16:32, BS:]]
            out_ref[pl.ds(pl.multiple_of(48 * g, 16), 48), :] = pack4(tiles)
            return 0

        lax.fori_loop(q * SHARE // 4, (q + 1) * SHARE // 4, group, 0, unroll=True)
    for copy in copies[REP:]:
        copy.wait()


def first_local_kernel(cols_ref, tracers_ref, wet_ref, coupling_ref, blocks_ref,
                       out_ref, far_ref, share_ref, wet_share_ref, coupling_out_ref,
                       wet_v, cols_s, tracers_v, near_ref, sems, block_sems):
    me = lax.axis_index("rep")
    cells = SHARE * BS
    copies = fetch([
        (cols_ref, cols_s), (tracers_ref, tracers_v),
        (tracers_ref.at[:, pl.ds(pl.multiple_of(me * cells, cells), cells)], share_ref),
        (wet_ref.at[pl.ds(pl.multiple_of(me * SHARE, SHARE), SHARE)], wet_v),
        (coupling_ref, coupling_out_ref),
    ], sems)
    block_copies = fetch_blocks(blocks_ref, near_ref, far_ref, block_sems)
    for copy in copies:
        copy.wait()
    wet_share_ref[...] = wet_v[...].astype(F32)

    def load_tile(i):
        return tile16(tracers_v[:, pl.ds(pl.multiple_of(i * BS, BS), BS)])

    local_groups(block_copies, cols_s, load_tile, near_ref, out_ref)


def second_local_kernel(cols_ref, table_ref, blocks_ref, out_ref, far_ref, cols_s, near_ref, sems, block_sems):
    copies = fetch([(cols_ref, cols_s)], sems)
    block_copies = fetch_blocks(blocks_ref, near_ref, far_ref, block_sems)
    copies[0].wait()
    local_groups(block_copies, cols_s, lambda i: table_ref[i], near_ref, out_ref)


def remote_groups(cols_ref, spots_ref, local_ref, far_ref, pieces, outs, cols_s, spots_s, table_ref, sems):
    me = lax.axis_index("rep")
    first_block = (lax.axis_index("blk") - 2) * NBD
    copies = fetch([(cols_ref, cols_s), (spots_ref, spots_s)], sems)

    for lane_no, piece in enumerate(pieces):

        def spread(g, _, lane_no=lane_no, piece=piece):
            rows = piece[pl.ds(pl.multiple_of(48 * g, 16), 48), :].astype(F32)
            for m, tile in enumerate(unpack4(rows)):
                table_ref[lane_no * CAP + 4 * g + m] = tile16(tile)
            return 0

        lax.fori_loop(0, CAP // 4, spread, 0, unroll=4)

    def tile(k, b):
        c = cols_s[k, b] - first_block
        return table_ref[spots_s[lax.shift_right_logical(c, 7), c & (NBD - 1)]]

    for copy in copies:
        copy.wait()
    for step, out_ref in enumerate(outs):
        share = me ^ step

        def group(g, _, out_ref=out_ref, share=share):
            tiles = []
            for pair in range(2):
                bs = [share * SHARE + 4 * g + 2 * pair + half for half in range(2)]
                x = [jnp.concatenate([tile(1, b), tile(2, b)], axis=1) for b in bs]
                w = [jnp.concatenate([far_ref[b, 0], far_ref[b, 1]], axis=1) for b in bs]
                y = nt(jnp.concatenate(x, axis=0), jnp.concatenate(w, axis=0))
                tiles += [y[0:16, 0:BS], y[16:32, BS:]]
            there = pl.ds(pl.multiple_of((share * (SHARE // 4) + g) * 48, 16), 48)
            total = pack4(tiles) + local_ref[there, :]
            out_ref[pl.ds(pl.multiple_of(48 * g, 16), 48), :] = total.astype(out_ref.dtype)
            return 0

        lax.fori_loop(0, SHARE // 4, group, 0, unroll=True)


def first_remote_kernel(cols_ref, local_ref, far_ref, p0, p1, p2, p3, own_ref, o1, o2, o3, ispots_ref,
                        cols_s, spots_s, table_ref, spots_v, sems):
    pieces = (p0, p1, p2, p3)
    spots_v[...] = jnp.zeros((8, BS), I32)
    ispots_ref[...] = jnp.zeros((8, BS), I32)
    message_spots(pieces, spots_v, ispots_ref)
    remote_groups(cols_ref, spots_v, local_ref, far_ref, pieces, (own_ref, o1, o2, o3),
                  cols_s, spots_s, table_ref, sems)


def second_remote_kernel(cols_ref, local_ref, far_ref, p0, p1, p2, p3, spots_ref, own_ref, o1, o2, o3,
                         cols_s, spots_s, table_ref, sems):
    remote_groups(cols_ref, spots_ref, local_ref, far_ref, (p0, p1, p2, p3), (own_ref, o1, o2, o3),
                  cols_s, spots_s, table_ref, sems)


def middle_kernel(own_ref, g1, g2, g3, share_ref, coupling_ref, wet_ref,
                  before_ref, packed_ref, mid_ref):
    for g in range(SHARE // 4):
        rows = pl.ds(48 * g, 48)
        total = own_ref[rows, :] + g1[rows, :].astype(F32) + g2[rows, :].astype(F32) + g3[rows, :].astype(F32)
        for m, tile in enumerate(unpack4(total)):
            lanes = pl.ds((4 * g + m) * BS, BS)
            mid_ref[:, lanes] = share_ref[:, lanes] + tile
    pushed = lax.dot_general(coupling_ref[...], mid_ref[...], (((1,), (0,)), ((), ())),
                             precision=lax.Precision.HIGHEST, preferred_element_type=F32)
    for g in range(SHARE // 4):
        tiles = []
        for m in range(4):
            b = 4 * g + m
            lanes = pl.ds(b * BS, BS)
            tile = mid_ref[:, lanes] + wet_ref[b : b + 1, :] * jnp.tanh(pushed[:, b * BS : (b + 1) * BS])
            before_ref[:, lanes] = tile
            tiles.append(tile)
        packed_ref[pl.ds(48 * g, 48), :] = pack4(tiles).astype(BF16)


def second_kernel(sends_ref, own, g2, g3, g1, *rest):
    outs, table_ref, sends_s, sems = rest[0:4], rest[4], rest[5], rest[6]
    copies = fetch([(sends_ref, sends_s)], sems)
    me = lax.axis_index("rep")
    for step, packed in ((0, own), (2, g2), (3, g3), (1, g1)):
        share = me ^ step

        def spread(g, _, packed=packed, share=share):
            rows = packed[pl.ds(pl.multiple_of(48 * g, 16), 48), :].astype(F32)
            for m, tile in enumerate(unpack4(rows)):
                table_ref[share * SHARE + 4 * g + m] = tile16(tile)
            return 0

        lax.fori_loop(0, SHARE // 4, spread, 0, unroll=4)
    copies[0].wait()
    gather_lists(sends_s, lambda i: table_ref[i].astype(F32), outs)


def last_kernel(own_ref, g1, g2, g3, before_ref, wet_ref, out_ref):
    for g in range(SHARE // 4):
        rows = pl.ds(48 * g, 48)
        total = own_ref[rows, :] + g1[rows, :].astype(F32) + g2[rows, :].astype(F32) + g3[rows, :].astype(F32)
        for m, tile in enumerate(unpack4(total)):
            b = 4 * g + m
            lanes = pl.ds(b * BS, BS)
            out_ref[:, lanes] = wet_ref[b : b + 1, :] * (before_ref[:, lanes] + tile)


def sds(shape, dtype):
    return jax.ShapeDtypeStruct(shape, dtype)


def call(body, outs, in_specs, scratch, name, mib, flops=0, bytes_accessed=0):
    kernel = pl.pallas_call(
        body,
        out_shape=outs,
        in_specs=in_specs,
        out_specs=jax.tree.map(lambda _: VMEM, outs),
        scratch_shapes=scratch,
        compiler_params=pltpu.CompilerParams(vmem_limit_bytes=mib * MIB),
        cost_estimate=pl.CostEstimate(flops=flops, bytes_accessed=bytes_accessed, transcendentals=0),
        name=name,
    )

    def run(*operands):
        return kernel(*(
            pltpu.with_memory_space_constraint(x, pltpu.HBM) if spec is HBM else x
            for x, spec in zip(operands, in_specs)))

    return run


def swap_blk(messages):
    n = lax.axis_size("blk")
    partners = (
        lambda i: i ^ 1,
        lambda i: i + 1 if i & 1 else i - 1,
        lambda i: i + 2 if i & 2 else i - 2,
        lambda i: i ^ 2,
    )
    return [
        lax.ppermute(x, "blk", [(i, to(i)) for i in range(n) if 0 <= to(i) < n])
        for x, to in zip(messages, partners)
    ]


def swap_rep(x, distance):
    n = lax.axis_size("rep")
    return lax.ppermute(x, "rep", [(i, i ^ distance) for i in range(n)])


def lists_out(label_rows):
    return [sds((LIST_ROWS + label_rows, BS), BF16)] * 4


def dma(n):
    return pltpu.SemaphoreType.DMA((n,))


FAR = pltpu.VMEM((NBD, 2, BS, BS), BF16)
NEAR = pltpu.VMEM((NBD, 1, BS, BS), BF16)
COLS = pltpu.SMEM((3, BS), I32)
SENDS = pltpu.SMEM((4, CAP), I32)


def on_device(tracers, explicit_blocks, explicit_cols, explicit_sends,
              implicit_blocks, implicit_cols, implicit_sends, coupling, wet):
    ecols, icols = explicit_cols.T, implicit_cols.T
    esends, isends = explicit_sends.reshape(4, CAP), implicit_sends.reshape(4, CAP)
    wet = wet.reshape(NBD, BS)
    cells = SHARE * BS
    ints = sds((8, BS), I32)
    sends_v = pltpu.VMEM((4, CAP), I32)
    local_sum = sds((NBD * NTR, BS), F32)
    part = sds((SHARE_ROWS, BS), BF16)
    parts_out = [sds((SHARE_ROWS, BS), F32), part, part, part]
    remote_scratch = [COLS, pltpu.SMEM((8, BS), I32), pltpu.VMEM((4 * CAP, 16, BS), BF16)]

    outbound = call(
        first_kernel, lists_out(LABEL_ROWS), [HBM] * 3,
        [sends_v, sends_v, SENDS, pltpu.VMEM((NTR, NBD * BS), F32), dma(4)],
        "first_lists", 16,
    )(esends, isends, tracers)
    pieces = swap_blk(outbound)
    local, far, share, wet_share, coupling = call(
        first_local_kernel,
        [local_sum, FAR, sds((NTR, cells), F32), sds((SHARE, BS), F32), sds((NTR, NTR), F32)], [HBM] * 5,
        [pltpu.VMEM((SHARE, BS), I32), COLS, pltpu.VMEM((NTR, NBD * BS), F32), NEAR, dma(5), dma(2 * REP)],
        "first_local_product", 24, flops=50_000_000, bytes_accessed=13_000_000,
    )(ecols, tracers, wet, coupling, explicit_blocks)
    own, *parts, ispots = call(
        first_remote_kernel, parts_out + [ints], [HBM] + [VMEM] * 6,
        remote_scratch + [pltpu.VMEM((8, BS), I32), dma(2)],
        "first_remote_product", 16, flops=100_000_000, bytes_accessed=1_000_000,
    )(ecols, local, far, *pieces)
    got = [swap_rep(parts[k - 1], k) for k in (1, 3, 2)]
    before, packed = call(
        middle_kernel, [sds((NTR, cells), F32), part], [VMEM] * 7, [pltpu.VMEM((NTR, cells), F32)],
        "middle", 16,
    )(own, *got, share, coupling, wet_share)
    others = [swap_rep(packed, k) for k in (2, 3, 1)]
    *outbound, table = call(
        second_kernel, lists_out(0) + [sds((NBD, 16, BS), BF16)], [HBM] + [VMEM] * 4, [SENDS, dma(1)],
        "second_lists", 16,
    )(isends, packed, *others)
    pieces = swap_blk(outbound)
    local, far = call(
        second_local_kernel, [local_sum, FAR], [HBM, VMEM, HBM], [COLS, NEAR, dma(1), dma(2 * REP)],
        "second_local_product", 24, flops=50_000_000, bytes_accessed=13_000_000,
    )(icols, table, implicit_blocks)
    own, *parts = call(
        second_remote_kernel, parts_out, [HBM] + [VMEM] * 7, remote_scratch + [dma(2)],
        "second_remote_product", 16, flops=100_000_000, bytes_accessed=1_000_000,
    )(icols, local, far, *pieces, ispots)
    got = [swap_rep(parts[k - 1], k) for k in (1, 3, 2)]
    return call(
        last_kernel, sds((NTR, cells), F32), [VMEM] * 6, [], "last", 16,
    )(own, *got, before, wet_share)


def solution(mesh):
    in_specs = (
        P(None, "blk"),
        P("blk", "rep", None, None),
        P("blk", "rep"),
        P("blk", "rep", None, None),
        P("blk", "rep", None, None),
        P("blk", "rep"),
        P("blk", "rep", None, None),
        P(),
        P("blk"),
    )
    out_specs = P(None, ("blk", "rep"))
    return jax.shard_map(
        on_device, mesh=mesh, in_specs=in_specs, out_specs=out_specs, check_vma=False
    )
```

```python
import jax
import jax.numpy as jnp
from jax import lax
from jax.experimental import pallas as pl
from jax.experimental.pallas import tpu as pltpu
from jax.sharding import PartitionSpec as P

NTR = 12
BS = 128
NBD = 128
CAP = 64
REP = 4
SHARE = NBD // REP
LIST_ROWS = CAP * NTR
LABEL_ROWS = 16
SHARE_ROWS = SHARE * NTR
FIRST_ORDER = (2, 3, 1, 0)
SECOND_ORDER = (2, 3, 1, 0)
FIRST_SUM = (2, 3, 1)
SECOND_SUM = (2, 3, 1)
GATHER = (1, 3, 2)
F32 = jnp.float32
BF16 = jnp.bfloat16
I32 = jnp.int32
MIB = 1 << 20

VMEM = pl.BlockSpec(memory_space=pltpu.VMEM)
HBM = pl.BlockSpec(memory_space=pltpu.HBM)


def nt(a, b):
    return lax.dot_general(a, b, (((1,), (1,)), ((), ())), preferred_element_type=F32)


def pack4(tiles):
    return jnp.concatenate([t[0:8] for t in tiles] + [t[8:12] for t in tiles], axis=0)


def unpack4(rows):
    return [
        jnp.concatenate([rows[8 * m : 8 * m + 8], rows[32 + 4 * m : 36 + 4 * m]], axis=0)
        for m in range(4)
    ]


def tile16(t):
    return jnp.concatenate([t, jnp.zeros((4, BS), F32)], axis=0).astype(BF16)


def route_lanes():
    me = lax.axis_index("blk")
    core = me & 1
    odd = lax.shift_right_logical(me, 1) & 1
    return (2 - core, 1 + core, 3 * odd, 3 - 3 * odd)


def message_spots(pieces, espots_ref, ispots_ref):
    me = lax.axis_index("blk")
    core = me & 1
    odd = lax.shift_right_logical(me, 1) & 1
    sub = lax.broadcasted_iota(I32, (BS, BS), 0).astype(F32)
    spot = lax.broadcasted_iota(I32, (8, BS), 1)
    kind = lax.broadcasted_iota(I32, (8, BS), 0)
    spot = jnp.where(lax.shift_right_logical(spot, 6) == kind, spot & (CAP - 1), 0)
    spot = spot.astype(F32).astype(BF16)
    for n, row in enumerate((3 - 2 * core, 1 + 2 * core, 4 * odd, 4 - 4 * odd)):
        labels = pieces[n][LIST_ROWS : LIST_ROWS + LABEL_ROWS, :].astype(F32)[0:1]
        listed = jnp.where(sub == labels, 1.0, 0.0).astype(BF16)
        found = nt(spot, listed).astype(I32) + n * CAP
        espots_ref[pl.ds(row, 1), :] = found[0:1]
        ispots_ref[pl.ds(row, 1), :] = found[1:2]


def gather_lists(order_ref, load_tile, out_refs):
    for lane_no, out_ref in zip(route_lanes(), out_refs):

        def group(g, _, lane_no=lane_no, out_ref=out_ref):
            tiles = [load_tile(jnp.maximum(order_ref[lane_no, 4 * g + m], 0)) for m in range(4)]
            rows = pl.ds(pl.multiple_of(48 * g, 16), 48)
            out_ref[rows, :] = pack4(tiles).astype(BF16)
            return 0

        lax.fori_loop(0, CAP // 4, group, 0, unroll=True)


def fetch(pairs, sems):
    copies = [pltpu.make_async_copy(src, dst, sems.at[n]) for n, (src, dst) in enumerate(pairs)]
    for copy in copies:
        copy.start()
    return copies


def first_kernel(esends_ref, isends_ref, tracers_ref, *rest):
    outs = rest[0:4]
    esends_v, isends_v, esends_s, tracers_v, sems = rest[4:]
    copies = fetch([(esends_ref, esends_s), (tracers_ref, tracers_v),
                    (esends_ref, esends_v), (isends_ref, isends_v)], sems)
    for copy in copies:
        copy.wait()
    for lane_no, out_ref in zip(route_lanes(), outs):
        row = pl.ds(lane_no, 1)
        labels = jnp.concatenate([esends_v[row, :], isends_v[row, :]], axis=1).astype(F32)
        out_ref[LIST_ROWS : LIST_ROWS + LABEL_ROWS, :] = jnp.broadcast_to(labels, (LABEL_ROWS, BS)).astype(BF16)

    def load_tile(i):
        return tracers_v[:, pl.ds(pl.multiple_of(i * BS, BS), BS)]

    gather_lists(esends_s, load_tile, outs)


def share_rows(n):
    return pl.ds(n * SHARE, SHARE)


STEPS = (1, 2, 3)


def fetch_blocks(blocks_ref, near_ref, far_ref, sems):
    me = lax.axis_index("rep")
    rows = [(share_rows(me ^ step), share_rows(n)) for n, step in enumerate(STEPS)]
    return fetch([(blocks_ref.at[r, pl.ds(0, 1)], near_ref.at[to]) for r, to in rows]
                 + [(blocks_ref.at[r, pl.ds(1, 2)], far_ref.at[to]) for r, to in rows], sems)


def packed_rows(n, g):
    return pl.ds(pl.multiple_of(n * SHARE_ROWS + 48 * g, 16), 48)


def local_groups(copies, cols_s, load_tile, near_ref, out_ref):
    me = lax.axis_index("rep")
    base = lax.axis_index("blk") * NBD
    for n, step in enumerate(STEPS):
        copies[n].wait()

        def group(g, _, n=n, step=step):
            tiles = []
            for pair in range(2):
                rows = [4 * g + 2 * pair + half for half in range(2)]
                x = [load_tile(cols_s[0, (me ^ step) * SHARE + row] - base) for row in rows]
                w = [near_ref[n * SHARE + row, 0] for row in rows]
                y = nt(jnp.concatenate(x, axis=0), jnp.concatenate(w, axis=0))
                tiles += [y[0:16, 0:BS], y[16:32, BS:]]
            out_ref[packed_rows(n, g), :] = pack4(tiles)
            return 0

        lax.fori_loop(0, SHARE // 4, group, 0, unroll=True)
    for copy in copies[len(STEPS):]:
        copy.wait()


def tracer_tile(tracers_v):
    return lambda i: tile16(tracers_v[:, pl.ds(pl.multiple_of(i * BS, BS), BS)])


def first_local_kernel(cols_ref, tracers_ref, wet_ref, coupling_ref, blocks_ref,
                       out_ref, far_ref, cols_v, share_ref, wet_share_ref, coupling_out_ref,
                       wet_v, cols_s, tracers_v, near_ref, sems, block_sems):
    me = lax.axis_index("rep")
    cells = SHARE * BS
    copies = fetch([
        (cols_ref, cols_s), (tracers_ref, tracers_v),
        (tracers_ref.at[:, pl.ds(pl.multiple_of(me * cells, cells), cells)], share_ref),
        (wet_ref.at[pl.ds(pl.multiple_of(me * SHARE, SHARE), SHARE)], wet_v),
        (coupling_ref, coupling_out_ref), (cols_ref, cols_v),
    ], sems)
    block_copies = fetch_blocks(blocks_ref, near_ref, far_ref, block_sems)
    for copy in copies:
        copy.wait()
    wet_share_ref[...] = wet_v[...].astype(F32)
    local_groups(block_copies, cols_s, tracer_tile(tracers_v), near_ref, out_ref)


def second_local_kernel(cols_ref, table_ref, blocks_ref, out_ref, far_ref, cols_v,
                        cols_s, near_ref, sems, block_sems):
    copies = fetch([(cols_ref, cols_s), (cols_ref, cols_v)], sems)
    block_copies = fetch_blocks(blocks_ref, near_ref, far_ref, block_sems)
    for copy in copies:
        copy.wait()
    local_groups(block_copies, cols_s, lambda i: table_ref[i], near_ref, out_ref)


def remote_tile(cols_s, spots_s, table_ref):
    first_block = (lax.axis_index("blk") - 2) * NBD

    def tile(k, b):
        c = cols_s[k, b] - first_block
        return table_ref[spots_s[lax.shift_right_logical(c, 7), c & (NBD - 1)]]

    return tile


def remote_groups(cols_ref, spots_ref, local_ref, far_ref, pieces, outs, table_ref, cols_s, spots_s, sems):
    me = lax.axis_index("rep")
    copies = fetch([(cols_ref, cols_s), (spots_ref, spots_s)], sems)

    for lane_no, piece in enumerate(pieces):

        def spread(g, _, lane_no=lane_no, piece=piece):
            rows = piece[pl.ds(pl.multiple_of(48 * g, 16), 48), :].astype(F32)
            for m, tile in enumerate(unpack4(rows)):
                table_ref[lane_no * CAP + 4 * g + m] = tile16(tile)
            return 0

        lax.fori_loop(0, CAP // 4, spread, 0, unroll=True)

    tile = remote_tile(cols_s, spots_s, table_ref)
    for copy in copies:
        copy.wait()
    for n, (step, out_ref) in enumerate(zip(STEPS, outs)):
        share = me ^ step

        def group(g, _, n=n, out_ref=out_ref, share=share):
            tiles = []
            for m in range(4):
                row = 4 * g + m
                b = share * SHARE + row
                h = n * SHARE + row
                x = jnp.concatenate([tile(1, b), tile(2, b)], axis=1)
                tiles.append(nt(x, jnp.concatenate([far_ref[h, 0], far_ref[h, 1]], axis=1)))
            total = pack4(tiles) + local_ref[packed_rows(n, g), :]
            out_ref[packed_rows(0, g), :] = total.astype(BF16)
            return 0

        lax.fori_loop(0, SHARE // 4, group, 0, unroll=True)


def in_order(pieces, order):
    return tuple(pieces[order.index(m)] for m in range(4))


def first_remote_kernel(cols_ref, local_ref, far_ref, p0, p1, p2, p3,
                        o1, o2, o3, table_ref, espots_ref, ispots_ref, cols_s, spots_s, sems):
    pieces = in_order((p0, p1, p2, p3), FIRST_ORDER)
    espots_ref[...] = jnp.zeros((8, BS), I32)
    ispots_ref[...] = jnp.zeros((8, BS), I32)
    message_spots(pieces, espots_ref, ispots_ref)
    remote_groups(cols_ref, espots_ref, local_ref, far_ref, pieces, (o1, o2, o3),
                  table_ref, cols_s, spots_s, sems)


def second_remote_kernel(cols_ref, local_ref, far_ref, p0, p1, p2, p3, spots_ref,
                         o1, o2, o3, table_ref, cols_s, spots_s, sems):
    pieces = in_order((p0, p1, p2, p3), SECOND_ORDER)
    remote_groups(cols_ref, spots_ref, local_ref, far_ref, pieces, (o1, o2, o3),
                  table_ref, cols_s, spots_s, sems)


def own_groups(cols_s, spots_s, load_tile, table_ref, held_ref, out_ref):
    me = lax.axis_index("rep")
    base = lax.axis_index("blk") * NBD
    tile = remote_tile(cols_s, spots_s, table_ref)

    def group(g, _):
        tiles = []
        for m in range(4):
            row = 4 * g + m
            b = me * SHARE + row
            x = jnp.concatenate([load_tile(cols_s[0, b] - base), tile(1, b), tile(2, b)], axis=1)
            tiles.append(nt(x, jnp.concatenate([held_ref[row, k] for k in range(3)], axis=1)))
        out_ref[packed_rows(0, g), :] = pack4(tiles)
        return 0

    lax.fori_loop(0, SHARE // 4, group, 0, unroll=True)


def first_own_kernel(cols_ref, spots_ref, blocks_ref, table_ref, tracers_ref,
                     out_ref, cols_s, spots_s, held_ref, tracers_v, sems):
    me = lax.axis_index("rep")
    copies = fetch([(cols_ref, cols_s), (spots_ref, spots_s), (tracers_ref, tracers_v),
                    (blocks_ref.at[share_rows(me)], held_ref)], sems)
    for copy in copies:
        copy.wait()
    own_groups(cols_s, spots_s, tracer_tile(tracers_v), table_ref, held_ref, out_ref)


def second_own_kernel(cols_ref, spots_ref, blocks_ref, table_ref, state_ref,
                      out_ref, cols_s, spots_s, held_ref, sems):
    me = lax.axis_index("rep")
    copies = fetch([(cols_ref, cols_s), (spots_ref, spots_s), (blocks_ref.at[share_rows(me)], held_ref)], sems)
    for copy in copies:
        copy.wait()
    own_groups(cols_s, spots_s, lambda i: state_ref[i], table_ref, held_ref, out_ref)


def middle_kernel(own_ref, g1, g2, g3, share_ref, coupling_ref, wet_ref,
                  before_ref, packed_ref, mid_ref):
    for g in range(SHARE // 4):
        rows = pl.ds(48 * g, 48)
        total = own_ref[rows, :] + g1[rows, :].astype(F32) + g2[rows, :].astype(F32) + g3[rows, :].astype(F32)
        for m, tile in enumerate(unpack4(total)):
            lanes = pl.ds((4 * g + m) * BS, BS)
            mid_ref[:, lanes] = share_ref[:, lanes] + tile
    pushed = lax.dot_general(coupling_ref[...], mid_ref[...], (((1,), (0,)), ((), ())),
                             precision=lax.Precision.HIGHEST, preferred_element_type=F32)
    for g in range(SHARE // 4):
        tiles = []
        for m in range(4):
            b = 4 * g + m
            lanes = pl.ds(b * BS, BS)
            tile = mid_ref[:, lanes] + wet_ref[b : b + 1, :] * jnp.tanh(pushed[:, b * BS : (b + 1) * BS])
            before_ref[:, lanes] = tile
            tiles.append(tile)
        packed_ref[pl.ds(48 * g, 48), :] = pack4(tiles).astype(BF16)


def second_kernel(sends_ref, own, ga, gb, gc, *rest):
    outs, table_ref, sends_s, sems = rest[0:4], rest[4], rest[5], rest[6]
    copies = fetch([(sends_ref, sends_s)], sems)
    me = lax.axis_index("rep")
    for step, packed in zip((0,) + GATHER, (own, ga, gb, gc)):
        share = me ^ step

        def spread(g, _, packed=packed, share=share):
            rows = packed[pl.ds(pl.multiple_of(48 * g, 16), 48), :].astype(F32)
            for m, tile in enumerate(unpack4(rows)):
                table_ref[share * SHARE + 4 * g + m] = tile16(tile)
            return 0

        lax.fori_loop(0, SHARE // 4, spread, 0, unroll=True)
    copies[0].wait()
    gather_lists(sends_s, lambda i: table_ref[i].astype(F32), outs)


def last_kernel(own_ref, g1, g2, g3, before_ref, wet_ref, out_ref):
    for g in range(SHARE // 4):
        rows = pl.ds(48 * g, 48)
        total = own_ref[rows, :] + g1[rows, :].astype(F32) + g2[rows, :].astype(F32) + g3[rows, :].astype(F32)
        for m, tile in enumerate(unpack4(total)):
            b = 4 * g + m
            lanes = pl.ds(b * BS, BS)
            out_ref[:, lanes] = wet_ref[b : b + 1, :] * (before_ref[:, lanes] + tile)


def sds(shape, dtype):
    return jax.ShapeDtypeStruct(shape, dtype)


def call(body, outs, in_specs, scratch, name, mib, flops=0, bytes_accessed=0):
    kernel = pl.pallas_call(
        body,
        out_shape=outs,
        in_specs=in_specs,
        out_specs=jax.tree.map(lambda _: VMEM, outs),
        scratch_shapes=scratch,
        compiler_params=pltpu.CompilerParams(vmem_limit_bytes=mib * MIB),
        cost_estimate=pl.CostEstimate(flops=flops, bytes_accessed=bytes_accessed, transcendentals=0),
        name=name,
    )

    def run(*operands):
        return kernel(*(
            pltpu.with_memory_space_constraint(x, pltpu.HBM) if spec is HBM else x
            for x, spec in zip(operands, in_specs)))

    return run


def swap_blk(messages):
    n = lax.axis_size("blk")
    partners = (
        lambda i: i ^ 1,
        lambda i: i + 1 if i & 1 else i - 1,
        lambda i: i + 2 if i & 2 else i - 2,
        lambda i: i ^ 2,
    )
    return [
        lax.ppermute(x, "blk", [(i, to(i)) for i in range(n) if 0 <= to(i) < n])
        for x, to in zip(messages, partners)
    ]


def swap_rep(x, distance):
    n = lax.axis_size("rep")
    return lax.ppermute(x, "rep", [(i, i ^ distance) for i in range(n)])


def lists_out(label_rows):
    return [sds((LIST_ROWS + label_rows, BS), BF16)] * 4


def dma(n):
    return pltpu.SemaphoreType.DMA((n,))


FAR = pltpu.VMEM((len(STEPS) * SHARE, 2, BS, BS), BF16)
NEAR = pltpu.VMEM((len(STEPS) * SHARE, 1, BS, BS), BF16)
HELD = pltpu.VMEM((SHARE, 3, BS, BS), BF16)
SPOTS = pltpu.SMEM((8, BS), I32)
STATE = pltpu.VMEM((NTR, NBD * BS), F32)
COLS = pltpu.SMEM((3, BS), I32)
SENDS = pltpu.SMEM((4, CAP), I32)


def on_device(tracers, explicit_blocks, explicit_cols, explicit_sends,
              implicit_blocks, implicit_cols, implicit_sends, coupling, wet):
    ecols, icols = explicit_cols.T, implicit_cols.T
    esends, isends = explicit_sends.reshape(4, CAP), implicit_sends.reshape(4, CAP)
    wet = wet.reshape(NBD, BS)
    cells = SHARE * BS
    ints = sds((8, BS), I32)
    sends_v = pltpu.VMEM((4, CAP), I32)
    local_sum = sds((len(STEPS) * SHARE_ROWS, BS), F32)
    cols_out = sds((3, BS), I32)
    own_sum = sds((SHARE_ROWS, BS), F32)
    part = sds((SHARE_ROWS, BS), BF16)
    parts_out = [part, part, part, sds((4 * CAP, 16, BS), BF16)]

    outbound = call(
        first_kernel, lists_out(LABEL_ROWS), [HBM] * 3,
        [sends_v, sends_v, SENDS, STATE, dma(4)],
        "first_lists", 16,
    )(esends, isends, tracers)
    pieces = swap_blk(outbound)
    local, far, cols_v, share, wet_share, coupling = call(
        first_local_kernel,
        [local_sum, FAR, cols_out, sds((NTR, cells), F32), sds((SHARE, BS), F32), sds((NTR, NTR), F32)],
        [HBM] * 5, [pltpu.VMEM((SHARE, BS), I32), COLS, STATE, NEAR, dma(6), dma(2 * len(STEPS))],
        "first_local_product", 24, flops=50_000_000, bytes_accessed=10_000_000,
    )(ecols, tracers, wet, coupling, explicit_blocks)
    *parts, far_table, espots, ispots = call(
        first_remote_kernel, parts_out + [ints, ints], [VMEM] * 7, [COLS, SPOTS, dma(2)],
        "first_remote_product", 16, flops=100_000_000, bytes_accessed=1_000_000,
    )(cols_v, local, far, *(pieces[m] for m in FIRST_ORDER))
    got = [swap_rep(parts[k - 1], k) for k in FIRST_SUM]
    own = call(
        first_own_kernel, own_sum, [VMEM, VMEM, HBM, VMEM, HBM], [COLS, SPOTS, HELD, STATE, dma(4)],
        "first_own_product", 16, flops=50_000_000, bytes_accessed=5_000_000,
    )(cols_v, espots, explicit_blocks, far_table, tracers)
    before, packed = call(
        middle_kernel, [sds((NTR, cells), F32), part], [VMEM] * 7, [pltpu.VMEM((NTR, cells), F32)],
        "middle", 16,
    )(own, *got, share, coupling, wet_share)
    others = [swap_rep(packed, k) for k in GATHER]
    *outbound, table = call(
        second_kernel, lists_out(0) + [sds((NBD, 16, BS), BF16)], [HBM] + [VMEM] * 4, [SENDS, dma(1)],
        "second_lists", 16,
    )(isends, packed, *others)
    pieces = swap_blk(outbound)
    local, far, cols_v = call(
        second_local_kernel, [local_sum, FAR, cols_out], [HBM, VMEM, HBM],
        [COLS, NEAR, dma(2), dma(2 * len(STEPS))],
        "second_local_product", 24, flops=50_000_000, bytes_accessed=10_000_000,
    )(icols, table, implicit_blocks)
    *parts, far_table = call(
        second_remote_kernel, parts_out, [VMEM] * 8, [COLS, SPOTS, dma(2)],
        "second_remote_product", 16, flops=100_000_000, bytes_accessed=1_000_000,
    )(cols_v, local, far, *(pieces[m] for m in SECOND_ORDER), ispots)
    got = [swap_rep(parts[k - 1], k) for k in SECOND_SUM]
    own = call(
        second_own_kernel, own_sum, [VMEM, VMEM, HBM, VMEM, VMEM], [COLS, SPOTS, HELD, dma(3)],
        "second_own_product", 16, flops=50_000_000, bytes_accessed=4_000_000,
    )(cols_v, ispots, implicit_blocks, far_table, table)
    return call(
        last_kernel, sds((NTR, cells), F32), [VMEM] * 6, [], "last", 16,
    )(own, *got, before, wet_share)


def solution(mesh):
    in_specs = (
        P(None, "blk"),
        P("blk", "rep", None, None),
        P("blk", "rep"),
        P("blk", "rep", None, None),
        P("blk", "rep", None, None),
        P("blk", "rep"),
        P("blk", "rep", None, None),
        P(),
        P("blk"),
    )
    out_specs = P(None, ("blk", "rep"))
    return jax.shard_map(
        on_device, mesh=mesh, in_specs=in_specs, out_specs=out_specs, check_vma=False
    )
```

```python
import jax
import jax.numpy as jnp
from jax import lax
from jax.experimental import pallas as pl
from jax.experimental.pallas import tpu as pltpu
from jax.sharding import PartitionSpec as P

NTR = 12
BS = 128
NBD = 128
CAP = 64
REP = 4
SHARE = NBD // REP
LIST_ROWS = CAP * NTR
LABEL_ROWS = 16
SHARE_ROWS = SHARE * NTR
FIRST_ORDER = (3, 2, 0, 1)
SECOND_ORDER = (3, 2, 0, 1)
LAST = 1
FIRST_SUM = (2, 3, 1)
SECOND_SUM = (2, 3, 1)
GATHER = (1, 3, 2)
F32 = jnp.float32
BF16 = jnp.bfloat16
I32 = jnp.int32
MIB = 1 << 20

VMEM = pl.BlockSpec(memory_space=pltpu.VMEM)
HBM = pl.BlockSpec(memory_space=pltpu.HBM)
PINNED = pl.BlockSpec(memory_space=pltpu.VMEM)


def nt(a, b):
    return lax.dot_general(a, b, (((1,), (1,)), ((), ())), preferred_element_type=F32)


def pack4(tiles):
    return jnp.concatenate([t[0:8] for t in tiles] + [t[8:12] for t in tiles], axis=0)


def unpack4(rows):
    return [
        jnp.concatenate([rows[8 * m : 8 * m + 8], rows[32 + 4 * m : 36 + 4 * m]], axis=0)
        for m in range(4)
    ]


def tile16(t):
    return jnp.concatenate([t, jnp.zeros((4, BS), F32)], axis=0).astype(BF16)


def route_lanes():
    me = lax.axis_index("blk")
    core = me & 1
    odd = lax.shift_right_logical(me, 1) & 1
    return (2 - core, 1 + core, 3 * odd, 3 - 3 * odd)


def message_spots(pieces, messages, espots_ref, ispots_ref):
    me = lax.axis_index("blk")
    core = me & 1
    odd = lax.shift_right_logical(me, 1) & 1
    sub = lax.broadcasted_iota(I32, (BS, BS), 0).astype(F32)
    spot = lax.broadcasted_iota(I32, (8, BS), 1)
    kind = lax.broadcasted_iota(I32, (8, BS), 0)
    spot = jnp.where(lax.shift_right_logical(spot, 6) == kind, spot & (CAP - 1), 0)
    spot = spot.astype(F32).astype(BF16)
    rows = (3 - 2 * core, 1 + 2 * core, 4 * odd, 4 - 4 * odd)
    for piece, n in zip(pieces, messages):
        row = rows[n]
        labels = piece[LIST_ROWS : LIST_ROWS + LABEL_ROWS, :].astype(F32)[0:1]
        listed = jnp.where(sub == labels, 1.0, 0.0).astype(BF16)
        found = nt(spot, listed).astype(I32) + n * CAP
        espots_ref[pl.ds(row, 1), :] = found[0:1]
        ispots_ref[pl.ds(row, 1), :] = found[1:2]


def gather_lists(order_ref, load_tile, out_refs):
    for lane_no, out_ref in zip(route_lanes(), out_refs):

        def group(g, _, lane_no=lane_no, out_ref=out_ref):
            tiles = [load_tile(jnp.maximum(order_ref[lane_no, 4 * g + m], 0)) for m in range(4)]
            rows = pl.ds(pl.multiple_of(48 * g, 16), 48)
            out_ref[rows, :] = pack4(tiles).astype(BF16)
            return 0

        lax.fori_loop(0, CAP // 4, group, 0, unroll=True)


def fetch(pairs, sems):
    copies = [pltpu.make_async_copy(src, dst, sems.at[n]) for n, (src, dst) in enumerate(pairs)]
    for copy in copies:
        copy.start()
    return copies


def first_kernel(esends_ref, isends_ref, tracers_ref, *rest):
    outs = rest[0:4]
    esends_v, isends_v, esends_s, tracers_v, sems = rest[4:]
    copies = fetch([(esends_ref, esends_s), (tracers_ref, tracers_v),
                    (esends_ref, esends_v), (isends_ref, isends_v)], sems)
    for copy in copies:
        copy.wait()
    for lane_no, out_ref in zip(route_lanes(), outs):
        row = pl.ds(lane_no, 1)
        labels = jnp.concatenate([esends_v[row, :], isends_v[row, :]], axis=1).astype(F32)
        out_ref[LIST_ROWS : LIST_ROWS + LABEL_ROWS, :] = jnp.broadcast_to(labels, (LABEL_ROWS, BS)).astype(BF16)

    def load_tile(i):
        return tracers_v[:, pl.ds(pl.multiple_of(i * BS, BS), BS)]

    gather_lists(esends_s, load_tile, outs)


def share_rows(n):
    return pl.ds(n * SHARE, SHARE)


STEPS = (1, 2, 3)


def packed_rows(n, g):
    return pl.ds(pl.multiple_of(n * SHARE_ROWS + 48 * g, 16), 48)


def local_groups(cols_s, load_tile, blocks_ref, out_ref):
    me = lax.axis_index("rep")
    base = lax.axis_index("blk") * NBD
    for n, step in enumerate(STEPS):

        def group(g, _, n=n, step=step):
            tiles = []
            for pair in range(2):
                rows = [4 * g + 2 * pair + half for half in range(2)]
                bs = [(me ^ step) * SHARE + row for row in rows]
                x = [load_tile(cols_s[0, b] - base) for b in bs]
                w = [blocks_ref[b, 0] for b in bs]
                y = nt(jnp.concatenate(x, axis=0), jnp.concatenate(w, axis=0))
                tiles += [y[0:16, 0:BS], y[16:32, BS:]]
            out_ref[packed_rows(n, g), :] = pack4(tiles)
            return 0

        lax.fori_loop(0, SHARE // 4, group, 0, unroll=True)


def tracer_tile(tracers_v):
    return lambda i: tile16(tracers_v[:, pl.ds(pl.multiple_of(i * BS, BS), BS)])


def first_local_kernel(cols_ref, tracers_ref, wet_ref, coupling_ref, blocks_ref,
                       out_ref, cols_v, share_ref, wet_share_ref, coupling_out_ref,
                       wet_v, cols_s, tracers_v, sems):
    me = lax.axis_index("rep")
    cells = SHARE * BS
    copies = fetch([
        (cols_ref, cols_s), (tracers_ref, tracers_v),
        (tracers_ref.at[:, pl.ds(pl.multiple_of(me * cells, cells), cells)], share_ref),
        (wet_ref.at[pl.ds(pl.multiple_of(me * SHARE, SHARE), SHARE)], wet_v),
        (coupling_ref, coupling_out_ref), (cols_ref, cols_v),
    ], sems)
    for copy in copies:
        copy.wait()
    wet_share_ref[...] = wet_v[...].astype(F32)
    local_groups(cols_s, tracer_tile(tracers_v), blocks_ref, out_ref)


def second_local_kernel(cols_ref, table_ref, blocks_ref, out_ref, cols_v, cols_s, sems):
    copies = fetch([(cols_ref, cols_s), (cols_ref, cols_v)], sems)
    for copy in copies:
        copy.wait()
    local_groups(cols_s, lambda i: table_ref[i], blocks_ref, out_ref)


def remote_tile(cols_s, spots_s, table_ref):
    first_block = (lax.axis_index("blk") - 2) * NBD

    def tile(k, b):
        c = cols_s[k, b] - first_block
        return table_ref[spots_s[lax.shift_right_logical(c, 7), c & (NBD - 1)]]

    return tile


def spread_pieces(pieces, messages, table_ref):
    for piece, message in zip(pieces, messages):

        def spread(g, _, message=message, piece=piece):
            rows = piece[pl.ds(pl.multiple_of(48 * g, 16), 48), :].astype(F32)
            for m, tile in enumerate(unpack4(rows)):
                table_ref[message * CAP + 4 * g + m] = tile16(tile)
            return 0

        lax.fori_loop(0, CAP // 4, spread, 0, unroll=True)


def remote_groups(cols_ref, spots_ref, local_ref, blocks_ref, piece, outs, table_ref, cols_s, spots_s, sems):
    me = lax.axis_index("rep")
    copies = fetch([(cols_ref, cols_s), (spots_ref, spots_s)], sems)
    spread_pieces((piece,), (LAST,), table_ref)
    tile = remote_tile(cols_s, spots_s, table_ref)
    for copy in copies:
        copy.wait()
    for n, (step, out_ref) in enumerate(zip(STEPS, outs)):
        share = me ^ step

        def group(g, _, n=n, out_ref=out_ref, share=share):
            tiles = []
            for m in range(4):
                row = 4 * g + m
                b = share * SHARE + row
                x = jnp.concatenate([tile(1, b), tile(2, b)], axis=1)
                tiles.append(nt(x, jnp.concatenate([blocks_ref[b, 1], blocks_ref[b, 2]], axis=1)))
            total = pack4(tiles) + local_ref[packed_rows(n, g), :]
            out_ref[packed_rows(0, g), :] = total.astype(BF16)
            return 0

        lax.fori_loop(0, SHARE // 4, group, 0, unroll=True)


def early(order):
    return tuple(m for m in order if m != LAST)


def first_spread_kernel(p0, p1, p2, table_ref, espots_ref, ispots_ref):
    messages = early(FIRST_ORDER)
    espots_ref[...] = jnp.zeros((8, BS), I32)
    ispots_ref[...] = jnp.zeros((8, BS), I32)
    message_spots((p0, p1, p2), messages, espots_ref, ispots_ref)
    spread_pieces((p0, p1, p2), messages, table_ref)


def second_spread_kernel(p0, p1, p2, table_ref):
    spread_pieces((p0, p1, p2), early(SECOND_ORDER), table_ref)


def first_remote_kernel(cols_ref, local_ref, blocks_ref, piece, table_in, espots_in, ispots_in,
                        o1, o2, o3, table_ref, espots_ref, ispots_ref, cols_s, spots_s, sems):
    espots_ref[...] = espots_in[...]
    ispots_ref[...] = ispots_in[...]
    message_spots((piece,), (LAST,), espots_ref, ispots_ref)
    remote_groups(cols_ref, espots_ref, local_ref, blocks_ref, piece, (o1, o2, o3),
                  table_ref, cols_s, spots_s, sems)


def second_remote_kernel(cols_ref, local_ref, blocks_ref, piece, table_in, spots_ref,
                         o1, o2, o3, table_ref, cols_s, spots_s, sems):
    remote_groups(cols_ref, spots_ref, local_ref, blocks_ref, piece, (o1, o2, o3),
                  table_ref, cols_s, spots_s, sems)


def own_groups(cols_s, spots_s, load_tile, table_ref, blocks_ref, out_ref):
    me = lax.axis_index("rep")
    base = lax.axis_index("blk") * NBD
    tile = remote_tile(cols_s, spots_s, table_ref)

    def group(g, _):
        tiles = []
        for m in range(4):
            row = 4 * g + m
            b = me * SHARE + row
            x = jnp.concatenate([load_tile(cols_s[0, b] - base), tile(1, b), tile(2, b)], axis=1)
            tiles.append(nt(x, jnp.concatenate([blocks_ref[b, k] for k in range(3)], axis=1)))
        out_ref[packed_rows(0, g), :] = pack4(tiles)
        return 0

    lax.fori_loop(0, SHARE // 4, group, 0, unroll=True)


def first_own_kernel(cols_ref, spots_ref, blocks_ref, table_ref, tracers_ref,
                     out_ref, cols_s, spots_s, tracers_v, sems):
    copies = fetch([(cols_ref, cols_s), (spots_ref, spots_s), (tracers_ref, tracers_v)], sems)
    for copy in copies:
        copy.wait()
    own_groups(cols_s, spots_s, tracer_tile(tracers_v), table_ref, blocks_ref, out_ref)


def second_own_kernel(cols_ref, spots_ref, blocks_ref, table_ref, state_ref,
                      out_ref, cols_s, spots_s, sems):
    copies = fetch([(cols_ref, cols_s), (spots_ref, spots_s)], sems)
    for copy in copies:
        copy.wait()
    own_groups(cols_s, spots_s, lambda i: state_ref[i], table_ref, blocks_ref, out_ref)


def middle_kernel(own_ref, g1, g2, g3, share_ref, coupling_ref, wet_ref,
                  before_ref, packed_ref, mid_ref):
    for g in range(SHARE // 4):
        rows = pl.ds(48 * g, 48)
        total = own_ref[rows, :] + g1[rows, :].astype(F32) + g2[rows, :].astype(F32) + g3[rows, :].astype(F32)
        for m, tile in enumerate(unpack4(total)):
            lanes = pl.ds((4 * g + m) * BS, BS)
            mid_ref[:, lanes] = share_ref[:, lanes] + tile
    pushed = lax.dot_general(coupling_ref[...], mid_ref[...], (((1,), (0,)), ((), ())),
                             precision=lax.Precision.HIGHEST, preferred_element_type=F32)
    for g in range(SHARE // 4):
        tiles = []
        for m in range(4):
            b = 4 * g + m
            lanes = pl.ds(b * BS, BS)
            tile = mid_ref[:, lanes] + wet_ref[b : b + 1, :] * jnp.tanh(pushed[:, b * BS : (b + 1) * BS])
            before_ref[:, lanes] = tile
            tiles.append(tile)
        packed_ref[pl.ds(48 * g, 48), :] = pack4(tiles).astype(BF16)


def second_kernel(sends_ref, own, ga, gb, gc, *rest):
    outs, table_ref, sends_s, sems = rest[0:4], rest[4], rest[5], rest[6]
    copies = fetch([(sends_ref, sends_s)], sems)
    me = lax.axis_index("rep")
    for step, packed in zip((0,) + GATHER, (own, ga, gb, gc)):
        share = me ^ step

        def spread(g, _, packed=packed, share=share):
            rows = packed[pl.ds(pl.multiple_of(48 * g, 16), 48), :].astype(F32)
            for m, tile in enumerate(unpack4(rows)):
                table_ref[share * SHARE + 4 * g + m] = tile16(tile)
            return 0

        lax.fori_loop(0, SHARE // 4, spread, 0, unroll=True)
    copies[0].wait()
    gather_lists(sends_s, lambda i: table_ref[i].astype(F32), outs)


def last_kernel(own_ref, g1, g2, g3, before_ref, wet_ref, out_ref, out_v, sems):
    copies = []
    for g in range(SHARE // 4):
        rows = pl.ds(48 * g, 48)
        total = own_ref[rows, :] + g1[rows, :].astype(F32) + g2[rows, :].astype(F32) + g3[rows, :].astype(F32)
        for m, tile in enumerate(unpack4(total)):
            b = 4 * g + m
            lanes = pl.ds(b * BS, BS)
            out_v[:, lanes] = wet_ref[b : b + 1, :] * (before_ref[:, lanes] + tile)
        if g % 2:
            lanes = pl.ds((g - 1) * 4 * BS, 8 * BS)
            copies.append(pltpu.make_async_copy(out_v.at[:, lanes], out_ref.at[:, lanes], sems.at[g // 2]))
            copies[-1].start()
    for copy in copies:
        copy.wait()


def sds(shape, dtype):
    return jax.ShapeDtypeStruct(shape, dtype)


def call(body, outs, in_specs, scratch, name, mib, flops=0, bytes_accessed=0, aliases=(), out_spec=VMEM):
    kernel = pl.pallas_call(
        body,
        out_shape=outs,
        in_specs=in_specs,
        out_specs=jax.tree.map(lambda _: out_spec, outs),
        scratch_shapes=scratch,
        input_output_aliases=dict(aliases),
        compiler_params=pltpu.CompilerParams(vmem_limit_bytes=mib * MIB),
        cost_estimate=pl.CostEstimate(flops=flops, bytes_accessed=bytes_accessed, transcendentals=0),
        name=name,
    )

    def run(*operands):
        return kernel(*(
            pltpu.with_memory_space_constraint(x, pltpu.HBM if spec is HBM else pltpu.VMEM)
            if spec is HBM else x
            for x, spec in zip(operands, in_specs)))

    return run


def swap_blk(messages):
    n = lax.axis_size("blk")
    partners = (
        lambda i: i ^ 1,
        lambda i: i + 1 if i & 1 else i - 1,
        lambda i: i + 2 if i & 2 else i - 2,
        lambda i: i ^ 2,
    )
    return [
        lax.ppermute(x, "blk", [(i, to(i)) for i in range(n) if 0 <= to(i) < n])
        for x, to in zip(messages, partners)
    ]


def swap_rep(x, distance):
    n = lax.axis_size("rep")
    return lax.ppermute(x, "rep", [(i, i ^ distance) for i in range(n)])


def lists_out(label_rows):
    return [sds((LIST_ROWS + label_rows, BS), BF16)] * 4


def dma(n):
    return pltpu.SemaphoreType.DMA((n,))


BLOCKS = pltpu.VMEM((NBD, 3, BS, BS), BF16)
SPOTS = pltpu.SMEM((8, BS), I32)
STATE = pltpu.VMEM((NTR, NBD * BS), F32)
COLS = pltpu.SMEM((3, BS), I32)
SENDS = pltpu.SMEM((4, CAP), I32)


def on_device(tracers, explicit_blocks, explicit_cols, explicit_sends,
              implicit_blocks, implicit_cols, implicit_sends, coupling, wet):
    ecols, icols = explicit_cols.T, implicit_cols.T
    esends, isends = explicit_sends.reshape(4, CAP), implicit_sends.reshape(4, CAP)
    wet = wet.reshape(NBD, BS)
    cells = SHARE * BS
    ints = sds((8, BS), I32)
    sends_v = pltpu.VMEM((4, CAP), I32)
    local_sum = sds((len(STEPS) * SHARE_ROWS, BS), F32)
    cols_out = sds((3, BS), I32)
    own_sum = sds((SHARE_ROWS, BS), F32)
    part = sds((SHARE_ROWS, BS), BF16)
    tiles = sds((4 * CAP, 16, BS), BF16)
    parts_out = [part, part, part, tiles]

    outbound = call(
        first_kernel, lists_out(LABEL_ROWS), [HBM] * 3,
        [sends_v, sends_v, SENDS, STATE, dma(4)],
        "first_lists", 16, flops=20_000_000_000, bytes_accessed=50_000_000,
    )(esends, isends, tracers)
    pieces = swap_blk(outbound)
    local, cols_v, share, wet_share, coupling = call(
        first_local_kernel,
        [local_sum, cols_out, sds((NTR, cells), F32), sds((SHARE, BS), F32), sds((NTR, NTR), F32)],
        [HBM] * 4 + [PINNED], [pltpu.VMEM((SHARE, BS), I32), COLS, STATE, dma(6)],
        "first_local_product", 16, flops=50_000_000, bytes_accessed=1_000_000,
    )(ecols, tracers, wet, coupling, explicit_blocks)
    far_table, espots, ispots = call(
        first_spread_kernel, [tiles, ints, ints], [VMEM] * 3, [], "first_spread", 8,
    )(*(pieces[m] for m in early(FIRST_ORDER)))
    *parts, far_table, espots, ispots = call(
        first_remote_kernel, parts_out + [ints, ints], [VMEM, VMEM, PINNED] + [VMEM] * 4, [COLS, SPOTS, dma(2)],
        "first_remote_product", 16, flops=100_000_000, bytes_accessed=1_000_000, aliases=((4, 3),),
    )(cols_v, local, explicit_blocks, pieces[LAST], far_table, espots, ispots)
    got = [swap_rep(parts[k - 1], k) for k in FIRST_SUM]
    own = call(
        first_own_kernel, own_sum, [VMEM, VMEM, PINNED, VMEM, HBM], [COLS, SPOTS, STATE, dma(3)],
        "first_own_product", 16, flops=50_000_000, bytes_accessed=1_000_000,
    )(cols_v, espots, explicit_blocks, far_table, tracers)
    before, packed = call(
        middle_kernel, [sds((NTR, cells), F32), part], [VMEM] * 7, [pltpu.VMEM((NTR, cells), F32)],
        "middle", 16,
    )(own, *got, share, coupling, wet_share)
    others = [swap_rep(packed, k) for k in GATHER]
    *outbound, table = call(
        second_kernel, lists_out(0) + [sds((NBD, 16, BS), BF16)], [HBM] + [VMEM] * 4, [SENDS, dma(1)],
        "second_lists", 16,
    )(isends, packed, *others)
    pieces = swap_blk(outbound)
    local, cols_v = call(
        second_local_kernel, [local_sum, cols_out], [HBM, VMEM, PINNED], [COLS, dma(2)],
        "second_local_product", 16, flops=50_000_000, bytes_accessed=1_000_000,
    )(icols, table, implicit_blocks)
    far_table = call(
        second_spread_kernel, tiles, [VMEM] * 3, [], "second_spread", 8,
    )(*(pieces[m] for m in early(SECOND_ORDER)))
    *parts, far_table = call(
        second_remote_kernel, parts_out, [VMEM, VMEM, PINNED] + [VMEM] * 3, [COLS, SPOTS, dma(2)],
        "second_remote_product", 16, flops=100_000_000, bytes_accessed=1_000_000, aliases=((4, 3),),
    )(cols_v, local, implicit_blocks, pieces[LAST], far_table, ispots)
    got = [swap_rep(parts[k - 1], k) for k in SECOND_SUM]
    own = call(
        second_own_kernel, own_sum, [VMEM, VMEM, PINNED, VMEM, VMEM], [COLS, SPOTS, dma(2)],
        "second_own_product", 16, flops=50_000_000, bytes_accessed=1_000_000,
    )(cols_v, ispots, implicit_blocks, far_table, table)
    return call(
        last_kernel, sds((NTR, cells), F32), [VMEM] * 6, [pltpu.VMEM((NTR, cells), F32), dma(SHARE // 8)],
        "last", 16, out_spec=HBM,
    )(own, *got, before, wet_share)


def solution(mesh):
    in_specs = (
        P(None, "blk"),
        P("blk", "rep", None, None),
        P("blk", "rep"),
        P("blk", "rep", None, None),
        P("blk", "rep", None, None),
        P("blk", "rep"),
        P("blk", "rep", None, None),
        P(),
        P("blk"),
    )
    out_specs = P(None, ("blk", "rep"))
    return jax.shard_map(
        on_device, mesh=mesh, in_specs=in_specs, out_specs=out_specs, check_vma=False
    )
```

```python
import jax
import jax.numpy as jnp
from jax import lax
from jax.experimental import pallas as pl
from jax.experimental.pallas import tpu as pltpu
from jax.sharding import PartitionSpec as P

NTR = 12
BS = 128
NBD = 128
CAP = 64
REP = 4
SHARE = NBD // REP
LIST_ROWS = CAP * NTR
LABEL_ROWS = 16
SHARE_ROWS = SHARE * NTR
FIRST_ORDER = (2, 3, 1, 0)
SECOND_ORDER = (2, 3, 0, 1)
FIRST_SUM = (2, 3, 1)
SECOND_SUM = (2, 3, 1)
GATHER = (1, 3, 2)
F32 = jnp.float32
BF16 = jnp.bfloat16
I32 = jnp.int32
MIB = 1 << 20

VMEM = pl.BlockSpec(memory_space=pltpu.VMEM)
HBM = pl.BlockSpec(memory_space=pltpu.HBM)


def nt(a, b):
    return lax.dot_general(a, b, (((1,), (1,)), ((), ())), preferred_element_type=F32)


def pack4(tiles):
    return jnp.concatenate([t[0:8] for t in tiles] + [t[8:12] for t in tiles], axis=0)


def unpack4(rows):
    return [
        jnp.concatenate([rows[8 * m : 8 * m + 8], rows[32 + 4 * m : 36 + 4 * m]], axis=0)
        for m in range(4)
    ]


def tile16(t):
    return jnp.concatenate([t, jnp.zeros((4, BS), F32)], axis=0).astype(BF16)


def route_lanes():
    me = lax.axis_index("blk")
    core = me & 1
    odd = lax.shift_right_logical(me, 1) & 1
    return (2 - core, 1 + core, 3 * odd, 3 - 3 * odd)


def message_spots(pieces, espots_ref, ispots_ref):
    me = lax.axis_index("blk")
    core = me & 1
    odd = lax.shift_right_logical(me, 1) & 1
    sub = lax.broadcasted_iota(I32, (BS, BS), 0).astype(F32)
    spot = lax.broadcasted_iota(I32, (8, BS), 1)
    kind = lax.broadcasted_iota(I32, (8, BS), 0)
    spot = jnp.where(lax.shift_right_logical(spot, 6) == kind, spot & (CAP - 1), 0)
    spot = spot.astype(F32).astype(BF16)
    for n, row in enumerate((3 - 2 * core, 1 + 2 * core, 4 * odd, 4 - 4 * odd)):
        labels = pieces[n][LIST_ROWS : LIST_ROWS + LABEL_ROWS, :].astype(F32)[0:1]
        listed = jnp.where(sub == labels, 1.0, 0.0).astype(BF16)
        found = nt(spot, listed).astype(I32) + n * CAP
        espots_ref[pl.ds(row, 1), :] = found[0:1]
        ispots_ref[pl.ds(row, 1), :] = found[1:2]


def gather_lists(order_ref, load_tile, out_refs):
    for lane_no, out_ref in zip(route_lanes(), out_refs):

        def group(g, _, lane_no=lane_no, out_ref=out_ref):
            tiles = [load_tile(jnp.maximum(order_ref[lane_no, 4 * g + m], 0)) for m in range(4)]
            rows = pl.ds(pl.multiple_of(48 * g, 16), 48)
            out_ref[rows, :] = pack4(tiles).astype(BF16)
            return 0

        lax.fori_loop(0, CAP // 4, group, 0, unroll=True)


def fetch(pairs, sems):
    copies = [pltpu.make_async_copy(src, dst, sems.at[n]) for n, (src, dst) in enumerate(pairs)]
    for copy in copies:
        copy.start()
    return copies


def first_kernel(esends_ref, isends_ref, tracers_ref, *rest):
    outs = rest[0:4]
    esends_v, isends_v, esends_s, tracers_v, sems = rest[4:]
    copies = fetch([(esends_ref, esends_s), (tracers_ref, tracers_v),
                    (esends_ref, esends_v), (isends_ref, isends_v)], sems)
    for copy in copies:
        copy.wait()
    for lane_no, out_ref in zip(route_lanes(), outs):
        row = pl.ds(lane_no, 1)
        labels = jnp.concatenate([esends_v[row, :], isends_v[row, :]], axis=1).astype(F32)
        out_ref[LIST_ROWS : LIST_ROWS + LABEL_ROWS, :] = jnp.broadcast_to(labels, (LABEL_ROWS, BS)).astype(BF16)

    def load_tile(i):
        return tracers_v[:, pl.ds(pl.multiple_of(i * BS, BS), BS)]

    gather_lists(esends_s, load_tile, outs)


def share_rows(n):
    return pl.ds(n * SHARE, SHARE)


STEPS = (1, 2, 3)


def fetch_blocks(blocks_ref, near_ref, far_ref, sems):
    me = lax.axis_index("rep")
    rows = [(share_rows(me ^ step), share_rows(n)) for n, step in enumerate(STEPS)]
    return fetch([(blocks_ref.at[r, pl.ds(0, 1)], near_ref.at[to]) for r, to in rows]
                 + [(blocks_ref.at[r, pl.ds(1, 2)], far_ref.at[to]) for r, to in rows], sems)


def packed_rows(n, g):
    return pl.ds(pl.multiple_of(n * SHARE_ROWS + 48 * g, 16), 48)


def local_groups(copies, cols_s, load_tile, near_ref, out_ref):
    me = lax.axis_index("rep")
    base = lax.axis_index("blk") * NBD
    for n, step in enumerate(STEPS):
        copies[n].wait()

        def group(g, _, n=n, step=step):
            tiles = []
            for pair in range(2):
                rows = [4 * g + 2 * pair + half for half in range(2)]
                x = [load_tile(cols_s[0, (me ^ step) * SHARE + row] - base) for row in rows]
                w = [near_ref[n * SHARE + row, 0] for row in rows]
                y = nt(jnp.concatenate(x, axis=0), jnp.concatenate(w, axis=0))
                tiles += [y[0:16, 0:BS], y[16:32, BS:]]
            out_ref[packed_rows(n, g), :] = pack4(tiles)
            return 0

        lax.fori_loop(0, SHARE // 4, group, 0, unroll=True)
    for copy in copies[len(STEPS):]:
        copy.wait()


def tracer_tile(tracers_v):
    return lambda i: tile16(tracers_v[:, pl.ds(pl.multiple_of(i * BS, BS), BS)])


def first_local_kernel(cols_ref, tracers_ref, wet_ref, coupling_ref, blocks_ref,
                       out_ref, far_ref, cols_v, share_ref, wet_share_ref, coupling_out_ref,
                       wet_v, cols_s, tracers_v, near_ref, sems, block_sems):
    me = lax.axis_index("rep")
    cells = SHARE * BS
    copies = fetch([
        (cols_ref, cols_s), (tracers_ref, tracers_v),
        (tracers_ref.at[:, pl.ds(pl.multiple_of(me * cells, cells), cells)], share_ref),
        (wet_ref.at[pl.ds(pl.multiple_of(me * SHARE, SHARE), SHARE)], wet_v),
        (coupling_ref, coupling_out_ref), (cols_ref, cols_v),
    ], sems)
    block_copies = fetch_blocks(blocks_ref, near_ref, far_ref, block_sems)
    for copy in copies:
        copy.wait()
    wet_share_ref[...] = wet_v[...].astype(F32)
    local_groups(block_copies, cols_s, tracer_tile(tracers_v), near_ref, out_ref)


def second_local_kernel(cols_ref, table_ref, blocks_ref, out_ref, far_ref, cols_v,
                        cols_s, near_ref, sems, block_sems):
    copies = fetch([(cols_ref, cols_s), (cols_ref, cols_v)], sems)
    block_copies = fetch_blocks(blocks_ref, near_ref, far_ref, block_sems)
    for copy in copies:
        copy.wait()
    local_groups(block_copies, cols_s, lambda i: table_ref[i], near_ref, out_ref)


def remote_tile(cols_s, spots_s, table_ref):
    first_block = (lax.axis_index("blk") - 2) * NBD

    def tile(k, b):
        c = cols_s[k, b] - first_block
        return table_ref[spots_s[lax.shift_right_logical(c, 7), c & (NBD - 1)]]

    return tile


def remote_groups(cols_ref, spots_ref, local_ref, far_ref, pieces, outs, table_ref, cols_s, spots_s, sems):
    me = lax.axis_index("rep")
    copies = fetch([(cols_ref, cols_s), (spots_ref, spots_s)], sems)

    for lane_no, piece in enumerate(pieces):

        def spread(g, _, lane_no=lane_no, piece=piece):
            rows = piece[pl.ds(pl.multiple_of(48 * g, 16), 48), :].astype(F32)
            for m, tile in enumerate(unpack4(rows)):
                table_ref[lane_no * CAP + 4 * g + m] = tile16(tile)
            return 0

        lax.fori_loop(0, CAP // 4, spread, 0, unroll=True)

    tile = remote_tile(cols_s, spots_s, table_ref)
    for copy in copies:
        copy.wait()
    for n, (step, out_ref) in enumerate(zip(STEPS, outs)):
        share = me ^ step

        def group(g, _, n=n, out_ref=out_ref, share=share):
            tiles = []
            for m in range(4):
                row = 4 * g + m
                b = share * SHARE + row
                h = n * SHARE + row
                x = jnp.concatenate([tile(1, b), tile(2, b)], axis=1)
                tiles.append(nt(x, jnp.concatenate([far_ref[h, 0], far_ref[h, 1]], axis=1)))
            total = pack4(tiles) + local_ref[packed_rows(n, g), :]
            out_ref[packed_rows(0, g), :] = total.astype(BF16)
            return 0

        lax.fori_loop(0, SHARE // 4, group, 0, unroll=True)


def in_order(pieces, order):
    return tuple(pieces[order.index(m)] for m in range(4))


def first_remote_kernel(cols_ref, local_ref, far_ref, p0, p1, p2, p3,
                        o1, o2, o3, table_ref, espots_ref, ispots_ref, cols_s, spots_s, sems):
    pieces = in_order((p0, p1, p2, p3), FIRST_ORDER)
    espots_ref[...] = jnp.zeros((8, BS), I32)
    ispots_ref[...] = jnp.zeros((8, BS), I32)
    message_spots(pieces, espots_ref, ispots_ref)
    remote_groups(cols_ref, espots_ref, local_ref, far_ref, pieces, (o1, o2, o3),
                  table_ref, cols_s, spots_s, sems)


def second_remote_kernel(cols_ref, local_ref, far_ref, p0, p1, p2, p3, spots_ref,
                         o1, o2, o3, table_ref, cols_s, spots_s, sems):
    pieces = in_order((p0, p1, p2, p3), SECOND_ORDER)
    remote_groups(cols_ref, spots_ref, local_ref, far_ref, pieces, (o1, o2, o3),
                  table_ref, cols_s, spots_s, sems)


def own_groups(cols_s, spots_s, load_tile, table_ref, held_ref, out_ref):
    me = lax.axis_index("rep")
    base = lax.axis_index("blk") * NBD
    tile = remote_tile(cols_s, spots_s, table_ref)

    def group(g, _):
        tiles = []
        for m in range(4):
            row = 4 * g + m
            b = me * SHARE + row
            x = jnp.concatenate([load_tile(cols_s[0, b] - base), tile(1, b), tile(2, b)], axis=1)
            tiles.append(nt(x, jnp.concatenate([held_ref[row, k] for k in range(3)], axis=1)))
        out_ref[packed_rows(0, g), :] = pack4(tiles)
        return 0

    lax.fori_loop(0, SHARE // 4, group, 0, unroll=True)


def first_own_kernel(cols_ref, spots_ref, blocks_ref, table_ref, tracers_ref,
                     out_ref, cols_s, spots_s, held_ref, tracers_v, sems):
    me = lax.axis_index("rep")
    copies = fetch([(cols_ref, cols_s), (spots_ref, spots_s), (tracers_ref, tracers_v),
                    (blocks_ref.at[share_rows(me)], held_ref)], sems)
    for copy in copies:
        copy.wait()
    own_groups(cols_s, spots_s, tracer_tile(tracers_v), table_ref, held_ref, out_ref)


def second_own_kernel(cols_ref, spots_ref, blocks_ref, table_ref, state_ref,
                      out_ref, cols_s, spots_s, held_ref, sems):
    me = lax.axis_index("rep")
    copies = fetch([(cols_ref, cols_s), (spots_ref, spots_s), (blocks_ref.at[share_rows(me)], held_ref)], sems)
    for copy in copies:
        copy.wait()
    own_groups(cols_s, spots_s, lambda i: state_ref[i], table_ref, held_ref, out_ref)


def middle_kernel(own_ref, g1, g2, g3, share_ref, coupling_ref, wet_ref,
                  before_ref, packed_ref, mid_ref):
    for g in range(SHARE // 4):
        rows = pl.ds(48 * g, 48)
        total = own_ref[rows, :] + g1[rows, :].astype(F32) + g2[rows, :].astype(F32) + g3[rows, :].astype(F32)
        for m, tile in enumerate(unpack4(total)):
            lanes = pl.ds((4 * g + m) * BS, BS)
            mid_ref[:, lanes] = share_ref[:, lanes] + tile
    pushed = lax.dot_general(coupling_ref[...], mid_ref[...], (((1,), (0,)), ((), ())),
                             precision=lax.Precision.HIGHEST, preferred_element_type=F32)
    for g in range(SHARE // 4):
        tiles = []
        for m in range(4):
            b = 4 * g + m
            lanes = pl.ds(b * BS, BS)
            tile = mid_ref[:, lanes] + wet_ref[b : b + 1, :] * jnp.tanh(pushed[:, b * BS : (b + 1) * BS])
            before_ref[:, lanes] = tile
            tiles.append(tile)
        packed_ref[pl.ds(48 * g, 48), :] = pack4(tiles).astype(BF16)


def second_kernel(sends_ref, own, ga, gb, gc, *rest):
    outs, table_ref, sends_s, sems = rest[0:4], rest[4], rest[5], rest[6]
    copies = fetch([(sends_ref, sends_s)], sems)
    me = lax.axis_index("rep")
    for step, packed in zip((0,) + GATHER, (own, ga, gb, gc)):
        share = me ^ step

        def spread(g, _, packed=packed, share=share):
            rows = packed[pl.ds(pl.multiple_of(48 * g, 16), 48), :].astype(F32)
            for m, tile in enumerate(unpack4(rows)):
                table_ref[share * SHARE + 4 * g + m] = tile16(tile)
            return 0

        lax.fori_loop(0, SHARE // 4, spread, 0, unroll=True)
    copies[0].wait()
    gather_lists(sends_s, lambda i: table_ref[i].astype(F32), outs)


def last_kernel(own_ref, g1, g2, g3, before_ref, wet_ref, out_ref):
    for g in range(SHARE // 4):
        rows = pl.ds(48 * g, 48)
        total = own_ref[rows, :] + g1[rows, :].astype(F32) + g2[rows, :].astype(F32) + g3[rows, :].astype(F32)
        for m, tile in enumerate(unpack4(total)):
            b = 4 * g + m
            lanes = pl.ds(b * BS, BS)
            out_ref[:, lanes] = wet_ref[b : b + 1, :] * (before_ref[:, lanes] + tile)


def sds(shape, dtype):
    return jax.ShapeDtypeStruct(shape, dtype)


def call(body, outs, in_specs, scratch, name, mib, flops=0, bytes_accessed=0):
    kernel = pl.pallas_call(
        body,
        out_shape=outs,
        in_specs=in_specs,
        out_specs=jax.tree.map(lambda _: VMEM, outs),
        scratch_shapes=scratch,
        compiler_params=pltpu.CompilerParams(vmem_limit_bytes=mib * MIB),
        cost_estimate=pl.CostEstimate(flops=flops, bytes_accessed=bytes_accessed, transcendentals=0),
        name=name,
    )

    def run(*operands):
        return kernel(*(
            pltpu.with_memory_space_constraint(x, pltpu.HBM) if spec is HBM else x
            for x, spec in zip(operands, in_specs)))

    return run


def swap_blk(messages):
    n = lax.axis_size("blk")
    partners = (
        lambda i: i ^ 1,
        lambda i: i + 1 if i & 1 else i - 1,
        lambda i: i + 2 if i & 2 else i - 2,
        lambda i: i ^ 2,
    )
    return [
        lax.ppermute(x, "blk", [(i, to(i)) for i in range(n) if 0 <= to(i) < n])
        for x, to in zip(messages, partners)
    ]


def swap_rep(x, distance):
    n = lax.axis_size("rep")
    return lax.ppermute(x, "rep", [(i, i ^ distance) for i in range(n)])


def lists_out(label_rows):
    return [sds((LIST_ROWS + label_rows, BS), BF16)] * 4


def dma(n):
    return pltpu.SemaphoreType.DMA((n,))


FAR = pltpu.VMEM((len(STEPS) * SHARE, 2, BS, BS), BF16)
NEAR = pltpu.VMEM((len(STEPS) * SHARE, 1, BS, BS), BF16)
HELD = pltpu.VMEM((SHARE, 3, BS, BS), BF16)
SPOTS = pltpu.SMEM((8, BS), I32)
STATE = pltpu.VMEM((NTR, NBD * BS), F32)
COLS = pltpu.SMEM((3, BS), I32)
SENDS = pltpu.SMEM((4, CAP), I32)


def on_device(tracers, explicit_blocks, explicit_cols, explicit_sends,
              implicit_blocks, implicit_cols, implicit_sends, coupling, wet):
    ecols, icols = explicit_cols.T, implicit_cols.T
    esends, isends = explicit_sends.reshape(4, CAP), implicit_sends.reshape(4, CAP)
    wet = wet.reshape(NBD, BS)
    cells = SHARE * BS
    ints = sds((8, BS), I32)
    sends_v = pltpu.VMEM((4, CAP), I32)
    local_sum = sds((len(STEPS) * SHARE_ROWS, BS), F32)
    cols_out = sds((3, BS), I32)
    own_sum = sds((SHARE_ROWS, BS), F32)
    part = sds((SHARE_ROWS, BS), BF16)
    parts_out = [part, part, part, sds((4 * CAP, 16, BS), BF16)]

    outbound = call(
        first_kernel, lists_out(LABEL_ROWS), [HBM] * 3,
        [sends_v, sends_v, SENDS, STATE, dma(4)],
        "first_lists", 16,
    )(esends, isends, tracers)
    pieces = swap_blk(outbound)
    local, far, cols_v, share, wet_share, coupling = call(
        first_local_kernel,
        [local_sum, FAR, cols_out, sds((NTR, cells), F32), sds((SHARE, BS), F32), sds((NTR, NTR), F32)],
        [HBM] * 5, [pltpu.VMEM((SHARE, BS), I32), COLS, STATE, NEAR, dma(6), dma(2 * len(STEPS))],
        "first_local_product", 24, flops=50_000_000, bytes_accessed=10_000_000,
    )(ecols, tracers, wet, coupling, explicit_blocks)
    *parts, far_table, espots, ispots = call(
        first_remote_kernel, parts_out + [ints, ints], [VMEM] * 7, [COLS, SPOTS, dma(2)],
        "first_remote_product", 16, flops=100_000_000, bytes_accessed=1_000_000,
    )(cols_v, local, far, *(pieces[m] for m in FIRST_ORDER))
    got = [swap_rep(parts[k - 1], k) for k in FIRST_SUM]
    own = call(
        first_own_kernel, own_sum, [VMEM, VMEM, HBM, VMEM, HBM], [COLS, SPOTS, HELD, STATE, dma(4)],
        "first_own_product", 16, flops=50_000_000, bytes_accessed=5_000_000,
    )(cols_v, espots, explicit_blocks, far_table, tracers)
    before, packed = call(
        middle_kernel, [sds((NTR, cells), F32), part], [VMEM] * 7, [pltpu.VMEM((NTR, cells), F32)],
        "middle", 16,
    )(own, *got, share, coupling, wet_share)
    others = [swap_rep(packed, k) for k in GATHER]
    *outbound, table = call(
        second_kernel, lists_out(0) + [sds((NBD, 16, BS), BF16)], [HBM] + [VMEM] * 4, [SENDS, dma(1)],
        "second_lists", 16,
    )(isends, packed, *others)
    pieces = swap_blk(outbound)
    local, far, cols_v = call(
        second_local_kernel, [local_sum, FAR, cols_out], [HBM, VMEM, HBM],
        [COLS, NEAR, dma(2), dma(2 * len(STEPS))],
        "second_local_product", 24, flops=50_000_000, bytes_accessed=10_000_000,
    )(icols, table, implicit_blocks)
    *parts, far_table = call(
        second_remote_kernel, parts_out, [VMEM] * 8, [COLS, SPOTS, dma(2)],
        "second_remote_product", 16, flops=100_000_000, bytes_accessed=1_000_000,
    )(cols_v, local, far, *(pieces[m] for m in SECOND_ORDER), ispots)
    got = [swap_rep(parts[k - 1], k) for k in SECOND_SUM]
    own = call(
        second_own_kernel, own_sum, [VMEM, VMEM, HBM, VMEM, VMEM], [COLS, SPOTS, HELD, dma(3)],
        "second_own_product", 16, flops=50_000_000, bytes_accessed=4_000_000,
    )(cols_v, ispots, implicit_blocks, far_table, table)
    return call(
        last_kernel, sds((NTR, cells), F32), [VMEM] * 6, [], "last", 16,
    )(own, *got, before, wet_share)


def solution(mesh):
    in_specs = (
        P(None, "blk"),
        P("blk", "rep", None, None),
        P("blk", "rep"),
        P("blk", "rep", None, None),
        P("blk", "rep", None, None),
        P("blk", "rep"),
        P("blk", "rep", None, None),
        P(),
        P("blk"),
    )
    out_specs = P(None, ("blk", "rep"))
    return jax.shard_map(
        on_device, mesh=mesh, in_specs=in_specs, out_specs=out_specs, check_vma=False
    )
```
